32 devices in a mesh: dp: 16 (over z, y, x), mp: 2 (over core).
Axes of the slice: x: 2, y: 2, z: 4, core: 2. Of those that a mesh axis runs over, the one named last changes fastest.
Arguments:
- hidden_in: bfloat16 [2048, 2048], P('dp'), may hold values from -6 to 6
- depth: int32 [2048], P('dp'), may hold values from 1 to 3
- destination: int32 [3, 2048], P(None, 'dp'), may hold values from 0 to 2047, as said below
- weight: bfloat16 [2048, 2048], P('dp', 'mp'), may hold values from -0.125 to 0.125
- cotangent: bfloat16 [2048, 2048], P('dp'), may hold values from -6 to 6
Outputs:
- final: bfloat16 [2048, 2048], P('dp')
- grad_in: bfloat16 [2048, 2048], P('dp')
- grad_weight: float32 [2048, 2048], P('dp', 'mp')
The draws below stay inside these ranges and needn't reach their ends.
Inputs may be any that keep to these rules, and one draw needn't show every extreme that they name: For each recursion, destination is a permutation of the 2048 rows; position p lies on device p // 128. The rows of one device go to 8 devices, exactly 16 rows to each.
All inputs are finite; a program needn't handle non-finite values.
Results may differ from the reference program's by a relative error of at most 0.017.
Values may be sent and summed in bfloat16 or wider, within the bound.
A program may use at most 128 MiB of HBM per device.

```python
import jax
import jax.numpy as jnp
from jax import lax

D = 2048
INNER = 2048
R_DEV = 128
NR = 2048
N_DP = 16
N_MP = 2


def draw_destination(key, part):
    key = jax.random.fold_in(key, 11)
    cap = max(2, 2 * R_DEV // N_DP)
    groups = R_DEV // cap
    tables = []
    for step in range(3):
        first, second, third = jax.random.split(jax.random.fold_in(key, step), 3)
        scores = jax.random.permutation(first, N_DP).astype(jnp.int32)
        scores = scores.at[N_DP - 1].set(-3).at[1].set(-2).at[N_DP // 2].set(-1)
        offsets = jnp.argsort(scores, stable=True).astype(jnp.int32)[:groups]
        base = jnp.tile(jnp.arange(R_DEV, dtype=jnp.int32)[None, :], (N_DP, 1))
        order = jax.random.permutation(second, base, axis=1, independent=True)
        slots = jax.random.permutation(third, base, axis=1, independent=True)
        position = jnp.arange(R_DEV, dtype=jnp.int32)
        group_of = position // cap
        source = jnp.arange(N_DP, dtype=jnp.int32)[:, None]
        target_dev = (source + offsets[group_of][None, :]) % N_DP
        within = jnp.broadcast_to(position[None, :], (N_DP, R_DEV))
        slot = slots[target_dev, within]
        value = target_dev * R_DEV + slot
        table = jnp.zeros((N_DP, R_DEV), jnp.int32).at[jnp.broadcast_to(source, (N_DP, R_DEV)), order].set(value)
        tables.append(table.reshape(-1))
    return jnp.stack(tables).astype(jnp.int32)


def touch_ends(array, key, low, top_value):
    shape = array.shape
    place = [jax.random.randint(jax.random.fold_in(key, axis), (), 0, shape[axis]) for axis in range(len(shape))]
    array = array.at[tuple(place)].set(low)
    longest = shape.index(max(shape))
    place[longest] = (place[longest] + 1) % shape[longest]
    return array.at[tuple(place)].set(top_value)


def raised(array, stream_key, source, target, shards_of, factor):
    owner, partner = [(jnp.arange(array.shape[axis_at]) // (array.shape[axis_at] // shards_of)).reshape([-1 if axis == axis_at else 1 for axis in range(array.ndim)]) for axis_at in (source, target)]
    chosen = jax.random.permutation(stream_key, shards_of)[partner]
    strong = (owner == chosen) | (owner == (partner + shards_of // 2) % shards_of)
    return jnp.where(strong, factor * array, array)


def block_levels(key, shape, cuts, low, top_value):
    level, own = 1.0, jax.random.fold_in(key, 6)
    for dim, parts in cuts:
        heights = jnp.exp(jax.random.uniform(jax.random.fold_in(own, dim), (parts,), jnp.float32, low / len(cuts), top_value / len(cuts)))
        level = level * jnp.repeat(heights, shape[dim] // parts).reshape([-1 if axis == dim else 1 for axis in range(len(shape))])
    return level


def scatter_about(key, dims, spread, reach, cuts=(), kind=jnp.bfloat16):
    result = jax.random.normal(key, dims, jnp.float32) * spread
    if len(cuts) > 0:
        result = block_levels(key, dims, cuts, -0.22, 0.18) * result
    return jnp.clip(result, min=-reach, max=reach).astype(kind)


def bell_draw_with(key, shape, deviation, most, shards, heavy, kind=jnp.bfloat16):
    drawn = deviation * jax.random.normal(key, shape, jnp.float32)
    if shards:
        drawn = drawn * block_levels(key, shape, shards, -0.22, 0.18)
    return jnp.clip(raised(drawn, jax.random.fold_in(key, 3), *heavy), -most, most).astype(kind)


def setup_inputs(seed: int = 0) -> dict:
    seeds = jax.random.split(jax.random.key(seed), 6)
    return {
        "hidden_in": scatter_about(seeds[0], (NR, D), 1.0, 6.0, ((0, 16),)),
        "depth": touch_ends(jax.random.randint(seeds[1], (NR,), 1, 4), jax.random.fold_in(seeds[1], 1), 1, 3).astype(jnp.int32),
        "destination": draw_destination(jax.random.fold_in(seeds[5], 71), 0),
        "weight": scatter_about(seeds[3], (D, INNER), D ** -0.5, 0.125, ((0, 16), (1, 2))),
        "cotangent": bell_draw_with(seeds[4], (NR, D), 1.0, 6.0, ((0, 16),), (0, 1, 16, 2.0)),
    }


def halves_product(left, weight):
    half = INNER // N_MP
    total = jnp.zeros((left.shape[0], weight.shape[0]), jnp.float32)
    for part_index in range(N_MP):
        term = jnp.dot(left[:, part_index * half:(part_index + 1) * half], weight[:, part_index * half:(part_index + 1) * half].T, preferred_element_type=jnp.float32)
        term = lax.optimization_barrier(term.astype(jnp.bfloat16))
        total = total + term.astype(jnp.float32)
    return total

def reference(hidden_in, depth, destination, weight, cotangent):
    state = hidden_in
    levels = depth
    saved = []
    for step in range(3):
        state = jnp.zeros_like(state).at[destination[step]].set(state)
        levels = jnp.zeros_like(levels).at[destination[step]].set(levels)
        state_f = state.astype(jnp.float32)
        rinv = lax.rsqrt(lax.optimization_barrier(jnp.mean(state_f * state_f, axis=-1, keepdims=True)) + 1e-06)
        normed = (state_f * rinv).astype(jnp.bfloat16)
        inner = jnp.dot(normed, weight, preferred_element_type=jnp.float32)
        gated = jax.nn.silu(inner).astype(jnp.bfloat16)
        branch = halves_product(gated, weight)
        active = (levels >= step + 1).astype(jnp.float32)[:, None]
        saved.append((state_f, rinv, normed, inner, gated, active))
        state = (state_f + active * branch).astype(jnp.bfloat16)
    final = state
    grad_state = cotangent.astype(jnp.float32)
    grad_weight = jnp.zeros((D, INNER), jnp.float32)
    for step in (2, 1, 0):
        state_f, rinv, normed, inner, gated, active = saved[step]
        grad_branch = (active * grad_state).astype(jnp.bfloat16)
        grad_gated = jnp.dot(grad_branch, weight, preferred_element_type=jnp.float32)
        sigma = jax.nn.sigmoid(inner)
        grad_inner = (grad_gated * sigma * (1.0 + inner * (1.0 - sigma))).astype(jnp.bfloat16)
        grad_normed = halves_product(grad_inner, weight)
        inner_mean = lax.optimization_barrier(jnp.mean(grad_normed * state_f, axis=-1, keepdims=True))
        grad_entry = grad_state + rinv * grad_normed - state_f * rinv * rinv * rinv * inner_mean
        grad_weight = grad_weight + jnp.dot(normed.T, grad_inner, preferred_element_type=jnp.float32) + jnp.dot(grad_branch.T, gated, preferred_element_type=jnp.float32)
        grad_state = grad_entry.astype(jnp.bfloat16)[destination[step]].astype(jnp.float32)
    return (final, grad_state.astype(jnp.bfloat16), grad_weight)
```

```python
import jax
import jax.numpy as jnp
from jax import lax
from jax.sharding import PartitionSpec as P


def pick(table, index):
    ids = lax.broadcasted_iota(jnp.int32, (index.shape[0], table.shape[0]), 1)
    return jnp.sum(jnp.where(ids == index[:, None], table[None, :], 0), axis=1)


def find(table, value):
    ids = lax.broadcasted_iota(jnp.int32, (value.shape[0], table.shape[0]), 1)
    return jnp.sum(jnp.where(table[None, :] == value[:, None], ids, 0), axis=1)


def take_rows(index, table):
    ids = lax.broadcasted_iota(jnp.int32, (index.shape[0], table.shape[0]), 1)
    return jnp.dot(
        (ids == index[:, None]).astype(jnp.bfloat16), table, preferred_element_type=jnp.float32
    ).astype(jnp.bfloat16)


def recursions(state, levels, cot, weight):
    saved = []
    for step in range(3):
        state_f = state.astype(jnp.float32)
        rinv = lax.rsqrt(jnp.mean(state_f * state_f, axis=-1, keepdims=True) + 1e-06)
        normed = (state_f * rinv).astype(jnp.bfloat16)
        inner = jnp.dot(normed, weight, preferred_element_type=jnp.float32)
        gated = jax.nn.silu(inner).astype(jnp.bfloat16)
        branch = lax.dot_general(
            gated, weight, (((1,), (1,)), ((), ())), preferred_element_type=jnp.float32
        )
        active = (levels >= step + 1).astype(jnp.float32)[:, None]
        saved.append((state_f, rinv, normed, inner, gated, active))
        state = (state_f + active * branch).astype(jnp.bfloat16)
    final = state
    grad = cot.astype(jnp.float32)
    lefts, rights = [], []
    for step in (2, 1, 0):
        state_f, rinv, normed, inner, gated, active = saved[step]
        grad_branch = (active * grad).astype(jnp.bfloat16)
        grad_gated = jnp.dot(grad_branch, weight, preferred_element_type=jnp.float32)
        sigma = jax.nn.sigmoid(inner)
        grad_inner = (grad_gated * sigma * (1.0 + inner * (1.0 - sigma))).astype(jnp.bfloat16)
        grad_normed = lax.dot_general(
            grad_inner, weight, (((1,), (1,)), ((), ())), preferred_element_type=jnp.float32
        )
        inner_mean = jnp.mean(grad_normed * state_f, axis=-1, keepdims=True)
        entry = grad + rinv * grad_normed - state_f * rinv * rinv * rinv * inner_mean
        lefts += [normed, grad_branch]
        rights += [grad_inner, gated]
        grad = entry.astype(jnp.bfloat16).astype(jnp.float32)
    return final, grad.astype(jnp.bfloat16), jnp.concatenate(lefts), jnp.concatenate(rights)


def body(hidden_in, depth, destination, weight, cotangent):
    rows, width = hidden_in.shape
    half_inner = weight.shape[1]
    cores = lax.axis_size("mp")
    me, core = lax.axis_index("dp"), lax.axis_index("mp")
    part, strip = rows // cores, width // cores
    columns = lax.all_gather(weight, "dp", axis=0, tiled=True)
    full = lax.all_gather(columns, "mp", axis=1, tiled=True)
    tables = lax.all_gather(destination, "dp", axis=1, tiled=True)
    cot_strip = lax.dynamic_slice_in_dim(cotangent, core * strip, strip, 1)
    cot_all = lax.all_gather(cot_strip, "dp", axis=0, tiled=True)
    place = pick(tables[2], pick(tables[1], destination[0]))
    own = me * rows + jnp.arange(rows, dtype=jnp.int32)
    source = find(tables[0], find(tables[1], find(tables[2], own)))
    cot_rows = lax.all_gather(take_rows(place, cot_all), "mp", axis=1, tiled=True)
    cot = lax.dynamic_slice_in_dim(cot_rows, core * part, part, 0)
    state = lax.dynamic_slice_in_dim(hidden_in, core * part, part, 0)
    levels = lax.dynamic_slice_in_dim(depth, core * part, part, 0)
    last, grad, left, right = recursions(state, levels, cot, full)
    last_all = lax.all_gather(last, "dp", axis=0, tiled=True)
    owner, offset = source // rows, source % rows
    slot = jnp.where(offset // part == core, owner * part + offset % part, -1)
    final = lax.psum(take_rows(slot, last_all), "mp")
    grad_in = lax.all_gather(grad, "mp", axis=0, tiled=True)
    left_all = lax.all_gather(left, "mp", axis=0, tiled=True)
    right_all = lax.all_gather(right, "mp", axis=0, tiled=True)
    right_half = lax.dynamic_slice_in_dim(right_all, core * half_inner, half_inner, 1)
    grad_weight = lax.dot_general(
        left_all, right_half, (((0,), (0,)), ((), ())), preferred_element_type=jnp.float32
    ).astype(jnp.bfloat16)
    owned = lax.psum_scatter(grad_weight, "dp", scatter_dimension=0, tiled=True)
    return final, grad_in, owned.astype(jnp.float32)


def solution(mesh):
    placed = (P("dp", None), P("dp"), P(None, "dp"), P("dp", "mp"), P("dp", None))
    return jax.shard_map(
        body,
        mesh=mesh,
        in_specs=placed,
        out_specs=(P("dp", None), P("dp", None), P("dp", "mp")),
        check_vma=False,
    )
```

```python
import jax
import jax.numpy as jnp
from jax import lax
from jax.experimental import pallas as pl
from jax.experimental.pallas import tpu as pltpu
from jax.sharding import PartitionSpec as P


MESH = pl.DeviceIdType.MESH


def push(src, dst, send, recv, device):
    copy = pltpu.make_async_remote_copy(
        src_ref=src,
        dst_ref=dst,
        send_sem=send,
        recv_sem=recv,
        device_id=device,
        device_id_type=MESH,
    )
    copy.start()


def landed(ref, recv):
    pltpu.make_async_copy(ref, ref, recv).wait()


def place_of(me):
    return me // 4, (me // 2) % 2, me % 2


def greet(z, y, x, core):
    barrier = pltpu.get_barrier_semaphore()

    def hello(device):
        pl.semaphore_signal(barrier, inc=1, device_id=device, device_id_type=MESH)

    me = z * 4 + y * 2 + x
    hello((me, 1 - core))
    hello((me + 1 - 2 * x, core))
    hello((me + 2 - 4 * y, core))

    @pl.when(z < 3)
    def _():
        hello((me + 4, core))

    @pl.when(z > 0)
    def _():
        hello((me - 4, core))

    pl.semaphore_wait(barrier, 3 + (1 - z // 3) + (z + 2) // 3)


def gather_kernel(
    block, out, local, zup, zdn, zrecv, asend, arecv, bsend, brecv, csend, crecv, cas, car, cbs, cbr
):
    me, core = lax.axis_index("dp"), lax.axis_index("mp")
    z, y, x = place_of(me)
    width = block.shape[1]
    half = width // 2
    base = pl.multiple_of(core * width, width)
    beside = (me, 1 - core)
    across = ((me + 1 - 2 * x, core), (me + 2 - 4 * y, core))
    greet(z, y, x, core)

    def cols(h):
        return pl.ds(pl.multiple_of(core * width + h * half, half), half)

    def whole(zp):
        return out.at[zp, y, x, :, pl.ds(base, width)]

    def piece(zp, yp, xp, h):
        return out.at[zp, yp, xp, :, cols(h)]

    def pair(zp, yp, xp, h):
        if h == 0:
            return out.at[zp, yp, :, :, cols(0)]
        return out.at[zp, :, xp, :, cols(1)]

    def spread(zp, source):
        for h in range(2):
            src = source.at[:, pl.ds(h * half, half)] if source is block else piece(zp, y, x, h)
            push(src, piece(zp, y, x, h), asend.at[h, zp], arecv.at[h, zp], across[h])
        push(source, whole(zp), csend.at[zp], crecv.at[zp], beside)

    def second(zp):
        for h in range(2):
            yp, xp = (y, 1 - x) if h == 0 else (1 - y, x)
            landed(piece(zp, yp, xp, h), arecv.at[h, zp])
            push(pair(zp, y, x, h), pair(zp, y, x, h), bsend.at[h, zp], brecv.at[h, zp], across[1 - h])
            push(piece(zp, yp, xp, h), piece(zp, yp, xp, h), cas.at[h, zp], car.at[h, zp], beside)

    def third(zp):
        for h in range(2):
            far = pair(zp, 1 - y, 1 - x, h)
            landed(far, brecv.at[h, zp])
            push(far, far, cbs.at[h, zp], cbr.at[h, zp], beside)

    def each(k, act):
        if k == 0:
            act(z)
            return

        @pl.when(z >= k)
        def _():
            act(z - k)

        @pl.when(z + k < 4)
        def _():
            act(z + k)

    own = pltpu.make_async_copy(block, whole(z), local)
    own.start()

    @pl.when(z < 3)
    def _():
        push(block, whole(z), zup.at[z], zrecv.at[z], (me + 4, core))

    @pl.when(z > 0)
    def _():
        push(block, whole(z), zdn.at[z], zrecv.at[z], (me - 4, core))

    spread(z, block)
    own.wait()
    for k in range(1, 4):

        @pl.when(z >= k)
        def _():
            zp = z - k
            landed(whole(zp), zrecv.at[zp])

            @pl.when(z < 3)
            def _():
                push(whole(zp), whole(zp), zup.at[zp], zrecv.at[zp], (me + 4, core))

            spread(zp, whole(zp))

        @pl.when(z + k < 4)
        def _():
            zp = z + k
            landed(whole(zp), zrecv.at[zp])

            @pl.when(z > 0)
            def _():
                push(whole(zp), whole(zp), zdn.at[zp], zrecv.at[zp], (me - 4, core))

            spread(zp, whole(zp))

        each(k - 1, second)
    each(3, second)
    for k in range(4):
        each(k, third)
    other = pl.multiple_of((1 - core) * width, width)

    def theirs(zp, yp, xp, h):
        return out.at[zp, yp, xp, :, pl.ds(pl.multiple_of(other + h * half, half), half)]

    def theirs_pair(zp, h):
        span = pl.ds(pl.multiple_of(other + h * half, half), half)
        if h == 0:
            return out.at[zp, 1 - y, :, :, span]
        return out.at[zp, :, 1 - x, :, span]

    for zp in range(4):
        landed(out.at[zp, y, x, :, pl.ds(other, width)], crecv.at[zp])
        landed(whole(zp), csend.at[zp])
        for h in range(2):
            yp, xp = (y, 1 - x) if h == 0 else (1 - y, x)
            landed(theirs(zp, yp, xp, h), car.at[h, zp])
            landed(theirs_pair(zp, h), cbr.at[h, zp])
            landed(piece(zp, y, x, h), asend.at[h, zp])
            landed(pair(zp, y, x, h), bsend.at[h, zp])
            landed(piece(zp, yp, xp, h), cas.at[h, zp])
            landed(pair(zp, 1 - y, 1 - x, h), cbs.at[h, zp])

        @pl.when((z < 3) & (zp <= z))
        def _():
            landed(whole(zp), zup.at[zp])

        @pl.when((z > 0) & (zp >= z))
        def _():
            landed(whole(zp), zdn.at[zp])


def gather_weight(block):
    rows, width = block.shape
    dma = pltpu.SemaphoreType.DMA
    out = pl.pallas_call(
        gather_kernel,
        out_shape=jax.ShapeDtypeStruct((4, 2, 2, rows, 2 * width), block.dtype),
        in_specs=[pl.BlockSpec(memory_space=pl.ANY)],
        out_specs=pl.BlockSpec(memory_space=pl.ANY),
        scratch_shapes=[
            dma(()),
            dma((4,)),
            dma((4,)),
            dma((4,)),
            dma((2, 4)),
            dma((2, 4)),
            dma((2, 4)),
            dma((2, 4)),
            dma((4,)),
            dma((4,)),
            dma((2, 4)),
            dma((2, 4)),
            dma((2, 4)),
            dma((2, 4)),
        ],
        compiler_params=pltpu.CompilerParams(collective_id=0, has_side_effects=True),
        cost_estimate=pl.CostEstimate(flops=0, bytes_accessed=100_000_000, transcendentals=0),
    )(block)
    return out.reshape(16 * rows, 2 * width)


def scatter_kernel(
    d, out, btake, agive, atake, total, ugive, utake, dgive, dtake,
    bsend, brecv, asend, arecv, usend, urecv, dsend, drecv,
):
    me, core = lax.axis_index("dp"), lax.axis_index("mp")
    z, y, x = place_of(me)
    half = d.shape[4] // 2
    across = ((me + 1 - 2 * x, core), (me + 2 - 4 * y, core))
    greet(z, y, x, core)
    first = 3 * (1 - z // 2)
    third = 1 + z % 2
    order = (first, 6 - first - third - z, third, z)

    def cols(h):
        return pl.ds(h * half, half)

    for zp in order:
        push(d.at[zp, 1 - y, :, :, cols(0)], btake.at[0, zp], bsend.at[0, zp], brecv.at[0, zp], across[1])
        push(d.at[zp, :, 1 - x, :, cols(1)], btake.at[1, zp], bsend.at[1, zp], brecv.at[1, zp], across[0])

    def wide(value):
        return value.astype(jnp.float32)

    def middle(zp):
        for h in range(2):
            yp, xp, far, near = (y, 1 - x, 1 - x, x) if h == 0 else (1 - y, x, 1 - y, y)
            landed(btake.at[h, zp], brecv.at[h, zp])
            agive[h, zp] = (wide(d[zp, yp, xp, :, cols(h)]) + wide(btake[h, zp, far])).astype(d.dtype)
            push(agive.at[h, zp], atake.at[h, zp], asend.at[h, zp], arecv.at[h, zp], across[h])
            total[h, zp] = wide(d[zp, y, x, :, cols(h)]) + wide(btake[h, zp, near])

    def line(zp):
        for h in range(2):
            landed(atake.at[h, zp], arecv.at[h, zp])
            total[h, zp] += wide(atake[h, zp])

            @pl.when(zp > z)
            def _():
                @pl.when(z > 0)
                def _():
                    landed(utake.at[h, zp], urecv.at[h, zp])
                    total[h, zp] += wide(utake[h, zp])

                ugive[h, zp] = total[h, zp].astype(d.dtype)
                push(ugive.at[h, zp], utake.at[h, zp], usend.at[h, zp], urecv.at[h, zp], (me + 4, core))

            @pl.when(zp < z)
            def _():
                @pl.when(z < 3)
                def _():
                    landed(dtake.at[h, zp], drecv.at[h, zp])
                    total[h, zp] += wide(dtake[h, zp])

                dgive[h, zp] = total[h, zp].astype(d.dtype)
                push(dgive.at[h, zp], dtake.at[h, zp], dsend.at[h, zp], drecv.at[h, zp], (me - 4, core))

    middle(order[0])
    for k in range(1, 4):
        middle(order[k])
        line(order[k - 1])
    line(z)
    for h in range(2):

        @pl.when(z > 0)
        def _():
            landed(utake.at[h, z], urecv.at[h, z])
            total[h, z] += wide(utake[h, z])

        @pl.when(z < 3)
        def _():
            landed(dtake.at[h, z], drecv.at[h, z])
            total[h, z] += wide(dtake[h, z])

        out[:, cols(h)] = total[h, z]
    for zp in range(4):
        for h in range(2):
            landed(btake.at[h, zp], bsend.at[h, zp])
            landed(atake.at[h, zp], asend.at[h, zp])

            @pl.when(zp > z)
            def _():
                landed(ugive.at[h, zp], usend.at[h, zp])

            @pl.when(zp < z)
            def _():
                landed(dgive.at[h, zp], dsend.at[h, zp])


def scatter_grad(partial):
    rows, width = partial.shape[0] // 16, partial.shape[1]
    half = width // 2
    dma = pltpu.SemaphoreType.DMA
    one = pltpu.VMEM((2, 4, rows, half), partial.dtype)
    return pl.pallas_call(
        scatter_kernel,
        out_shape=jax.ShapeDtypeStruct((rows, width), jnp.float32),
        in_specs=[pl.BlockSpec(memory_space=pltpu.VMEM)],
        out_specs=pl.BlockSpec(memory_space=pltpu.VMEM),
        scratch_shapes=[
            pltpu.VMEM((2, 4, 2, rows, half), partial.dtype),
            one,
            one,
            pltpu.VMEM((2, 4, rows, half), jnp.float32),
            one,
            one,
            one,
            one,
        ]
        + [dma((2, 4))] * 8,
        compiler_params=pltpu.CompilerParams(
            collective_id=1, has_side_effects=True, vmem_limit_bytes=32 * 1024 * 1024
        ),
        cost_estimate=pl.CostEstimate(flops=0, bytes_accessed=100_000_000, transcendentals=0),
    )(partial.reshape(4, 2, 2, rows, width))


def pick(table, index):
    ids = lax.broadcasted_iota(jnp.int32, (index.shape[0], table.shape[0]), 1)
    return jnp.sum(jnp.where(ids == index[:, None], table[None, :], 0), axis=1)


def find(table, value):
    ids = lax.broadcasted_iota(jnp.int32, (value.shape[0], table.shape[0]), 1)
    return jnp.sum(jnp.where(table[None, :] == value[:, None], ids, 0), axis=1)


def take_rows(index, table):
    ids = lax.broadcasted_iota(jnp.int32, (index.shape[0], table.shape[0]), 1)
    return jnp.dot(
        (ids == index[:, None]).astype(jnp.bfloat16), table, preferred_element_type=jnp.float32
    ).astype(jnp.bfloat16)


def recursions(state, levels, cot, weight):
    saved = []
    for step in range(3):
        state_f = state.astype(jnp.float32)
        rinv = lax.rsqrt(jnp.mean(state_f * state_f, axis=-1, keepdims=True) + 1e-06)
        normed = (state_f * rinv).astype(jnp.bfloat16)
        inner = jnp.dot(normed, weight, preferred_element_type=jnp.float32)
        gated = jax.nn.silu(inner).astype(jnp.bfloat16)
        branch = lax.dot_general(
            gated, weight, (((1,), (1,)), ((), ())), preferred_element_type=jnp.float32
        )
        active = (levels >= step + 1).astype(jnp.float32)[:, None]
        saved.append((state_f, rinv, normed, inner, gated, active))
        state = (state_f + active * branch).astype(jnp.bfloat16)
    final = state
    grad = cot.astype(jnp.float32)
    lefts, rights = [], []
    for step in (2, 1, 0):
        state_f, rinv, normed, inner, gated, active = saved[step]
        grad_branch = (active * grad).astype(jnp.bfloat16)
        grad_gated = jnp.dot(grad_branch, weight, preferred_element_type=jnp.float32)
        sigma = jax.nn.sigmoid(inner)
        grad_inner = (grad_gated * sigma * (1.0 + inner * (1.0 - sigma))).astype(jnp.bfloat16)
        grad_normed = lax.dot_general(
            grad_inner, weight, (((1,), (1,)), ((), ())), preferred_element_type=jnp.float32
        )
        inner_mean = jnp.mean(grad_normed * state_f, axis=-1, keepdims=True)
        entry = grad + rinv * grad_normed - state_f * rinv * rinv * rinv * inner_mean
        lefts += [normed, grad_branch]
        rights += [grad_inner, gated]
        grad = entry.astype(jnp.bfloat16).astype(jnp.float32)
    return final, grad.astype(jnp.bfloat16), jnp.concatenate(lefts), jnp.concatenate(rights)


def body(hidden_in, depth, destination, weight, cotangent):
    rows, width = hidden_in.shape
    half_inner = weight.shape[1]
    cores = lax.axis_size("mp")
    me, core = lax.axis_index("dp"), lax.axis_index("mp")
    part, strip = rows // cores, width // cores
    square = lax.axis_size("dp") == 16 and cores == 2
    if square:
        full = gather_weight(weight)
    else:
        columns = lax.all_gather(weight, "dp", axis=0, tiled=True)
        full = lax.all_gather(columns, "mp", axis=1, tiled=True)
    tables = lax.all_gather(destination, "dp", axis=1, tiled=True)
    cot_strip = lax.dynamic_slice_in_dim(cotangent, core * strip, strip, 1)
    cot_all = lax.all_gather(cot_strip, "dp", axis=0, tiled=True)
    place = pick(tables[2], pick(tables[1], destination[0]))
    own = me * rows + jnp.arange(rows, dtype=jnp.int32)
    source = find(tables[0], find(tables[1], find(tables[2], own)))
    cot_rows = lax.all_gather(take_rows(place, cot_all), "mp", axis=1, tiled=True)
    cot = lax.dynamic_slice_in_dim(cot_rows, core * part, part, 0)
    state = lax.dynamic_slice_in_dim(hidden_in, core * part, part, 0)
    levels = lax.dynamic_slice_in_dim(depth, core * part, part, 0)
    last, grad, left, right = recursions(state, levels, cot, full)
    last_all = lax.all_gather(last, "dp", axis=0, tiled=True)
    owner, offset = source // rows, source % rows
    slot = jnp.where(offset // part == core, owner * part + offset % part, -1)
    final = lax.psum(take_rows(slot, last_all), "mp")
    grad_in = lax.all_gather(grad, "mp", axis=0, tiled=True)
    left_all = lax.all_gather(left, "mp", axis=0, tiled=True)
    right_all = lax.all_gather(right, "mp", axis=0, tiled=True)
    right_half = lax.dynamic_slice_in_dim(right_all, core * half_inner, half_inner, 1)
    grad_weight = lax.dot_general(
        left_all, right_half, (((0,), (0,)), ((), ())), preferred_element_type=jnp.float32
    ).astype(jnp.bfloat16)
    if square:
        return final, grad_in, scatter_grad(grad_weight)
    owned = lax.psum_scatter(grad_weight, "dp", scatter_dimension=0, tiled=True)
    return final, grad_in, owned.astype(jnp.float32)


def solution(mesh):
    placed = (P("dp", None), P("dp"), P(None, "dp"), P("dp", "mp"), P("dp", None))
    return jax.shard_map(
        body,
        mesh=mesh,
        in_specs=placed,
        out_specs=(P("dp", None), P("dp", None), P("dp", "mp")),
        check_vma=False,
    )
```

```python
import jax
import jax.numpy as jnp
from jax import lax
from jax.experimental import pallas as pl
from jax.experimental.pallas import tpu as pltpu
from jax.sharding import PartitionSpec as P


MESH = pl.DeviceIdType.MESH
TILE = 512


def push(src, dst, send, recv, device):
    copy = pltpu.make_async_remote_copy(
        src_ref=src,
        dst_ref=dst,
        send_sem=send,
        recv_sem=recv,
        device_id=device,
        device_id_type=MESH,
    )
    copy.start()


def landed(ref, recv):
    pltpu.make_async_copy(ref, ref, recv).wait()


def place_of(me):
    return me // 4, (me // 2) % 2, me % 2


def greet(z, y, x, core):
    barrier = pltpu.get_barrier_semaphore()

    def hello(device):
        pl.semaphore_signal(barrier, inc=1, device_id=device, device_id_type=MESH)

    me = z * 4 + y * 2 + x
    hello((me, 1 - core))
    hello((me + 1 - 2 * x, core))
    hello((me + 2 - 4 * y, core))

    @pl.when(z < 3)
    def _():
        hello((me + 4, core))

    @pl.when(z > 0)
    def _():
        hello((me - 4, core))

    pl.semaphore_wait(barrier, 3 + (1 - z // 3) + (z + 2) // 3)


class Relay:
    def __init__(self, block, out, sems, paths=(0, 1), beside=False):
        self.block, self.out, self.sems, self.paths, self.beside = block, out, sems, paths, beside
        self.me, self.core = lax.axis_index("dp"), lax.axis_index("mp")
        self.z, self.y, self.x = place_of(self.me)
        self.width = block.shape[1]
        self.half = self.width // len(paths)
        self.sibling = (self.me, 1 - self.core)
        me, x, y = self.me, self.x, self.y
        self.across = ((me + 1 - 2 * x, self.core), (me + 2 - 4 * y, self.core))

    def span(self, h, core=None):
        core = self.core if core is None else core
        if not self.beside:
            return pl.ds(h * self.half, self.half)
        return pl.ds(pl.multiple_of(core * self.width + h * self.half, self.half), self.half)

    def whole(self, zp, core=None):
        core = self.core if core is None else core
        if not self.beside:
            return self.out.at[zp, self.y, self.x]
        start = pl.multiple_of(core * self.width, self.width)
        return self.out.at[zp, self.y, self.x, :, pl.ds(start, self.width)]

    def piece(self, zp, far, h, core=None):
        x, y = self.x, self.y
        if far:
            x, y = (1 - x, y) if h == 0 else (x, 1 - y)
        return self.out.at[zp, y, x, :, self.span(h, core)]

    def pair(self, zp, far, h, core=None):
        if h == 0:
            y = 1 - self.y if far else self.y
            return self.out.at[zp, y, :, :, self.span(0, core)]
        x = 1 - self.x if far else self.x
        return self.out.at[zp, :, x, :, self.span(1, core)]

    def spread(self, zp, own):
        asend, arecv = self.sems[4:6]
        for h in self.paths:
            src = self.piece(zp, False, h)
            if own:
                src = self.block.at[:, pl.ds(h * self.half, self.half)]
            push(src, self.piece(zp, False, h), asend.at[h, zp], arecv.at[h, zp], self.across[h])
        if self.beside:
            csend, crecv = self.sems[8:10]
            src = self.block if own else self.whole(zp)
            push(src, self.whole(zp), csend.at[zp], crecv.at[zp], self.sibling)

    def second(self, zp):
        arecv, bsend, brecv = self.sems[5:8]
        for h in self.paths:
            got, both = self.piece(zp, True, h), self.pair(zp, False, h)
            landed(got, arecv.at[h, zp])
            push(both, both, bsend.at[h, zp], brecv.at[h, zp], self.across[1 - h])
            if self.beside:
                cas, car = self.sems[10:12]
                push(got, got, cas.at[h, zp], car.at[h, zp], self.sibling)

    def third(self, zp):
        for h in self.paths:
            got = self.pair(zp, True, h)
            landed(got, self.sems[7].at[h, zp])
            if self.beside:
                cbs, cbr = self.sems[12:14]
                push(got, got, cbs.at[h, zp], cbr.at[h, zp], self.sibling)

    def each(self, k, act):
        z = self.z
        if k == 0:
            act(z)
            return

        @pl.when(z >= k)
        def _():
            act(z - k)

        @pl.when(z + k < 4)
        def _():
            act(z + k)

    def up(self, zp, src):
        zup, zrecv = self.sems[1], self.sems[3]

        @pl.when(self.z < 3)
        def _():
            push(src, self.whole(zp), zup.at[zp], zrecv.at[zp], (self.me + 4, self.core))

    def down(self, zp, src):
        zdn, zrecv = self.sems[2], self.sems[3]

        @pl.when(self.z > 0)
        def _():
            push(src, self.whole(zp), zdn.at[zp], zrecv.at[zp], (self.me - 4, self.core))

    def start(self):
        z = self.z
        own = pltpu.make_async_copy(self.block, self.whole(z), self.sems[0])
        own.start()
        self.up(z, self.block)
        self.down(z, self.block)
        self.spread(z, True)
        own.wait()

    def step(self, k):
        z = self.z

        @pl.when(z >= k)
        def _():
            zp = z - k
            landed(self.whole(zp), self.sems[3].at[zp])
            self.up(zp, self.whole(zp))
            self.spread(zp, False)

        @pl.when(z + k < 4)
        def _():
            zp = z + k
            landed(self.whole(zp), self.sems[3].at[zp])
            self.down(zp, self.whole(zp))
            self.spread(zp, False)

        self.each(k - 1, self.second)

    def finish(self):
        self.each(3, self.second)
        for k in range(4):
            self.each(k, self.third)
        z, other = self.z, 1 - self.core
        for zp in range(4):
            for h in self.paths:
                landed(self.piece(zp, False, h), self.sems[4].at[h, zp])
                landed(self.pair(zp, False, h), self.sems[6].at[h, zp])
            if self.beside:
                csend, crecv, cas, car, cbs, cbr = self.sems[8:14]
                landed(self.whole(zp, other), crecv.at[zp])
                landed(self.whole(zp), csend.at[zp])
                for h in self.paths:
                    landed(self.piece(zp, True, h, other), car.at[h, zp])
                    landed(self.pair(zp, True, h, other), cbr.at[h, zp])
                    landed(self.piece(zp, True, h), cas.at[h, zp])
                    landed(self.pair(zp, True, h), cbs.at[h, zp])

            @pl.when((z < 3) & (zp <= z))
            def _():
                landed(self.whole(zp), self.sems[1].at[zp])

            @pl.when((z > 0) & (zp >= z))
            def _():
                landed(self.whole(zp), self.sems[2].at[zp])


def relay_sems(beside):
    dma = pltpu.SemaphoreType.DMA
    base = [dma(()), dma((4,)), dma((4,)), dma((4,))] + [dma((2, 4))] * 4
    return base + ([dma((4,)), dma((4,))] + [dma((2, 4))] * 4 if beside else [])


def enter():
    me, core = lax.axis_index("dp"), lax.axis_index("mp")
    greet(*place_of(me), core)


def gather_kernel(block, table, out, tables, *sems):
    main = Relay(block, out, sems[:14], beside=True)
    small = Relay(table, tables, sems[14:], paths=(0,))
    enter()
    main.start()
    small.start()
    for k in range(1, 4):
        main.step(k)
        small.step(k)
    small.finish()
    main.finish()


def params(number):
    return pltpu.CompilerParams(
        collective_id=number, has_side_effects=True, vmem_limit_bytes=48 * 1024 * 1024
    )


def gather_weight(block, table):
    rows, width = block.shape
    anywhere = pl.BlockSpec(memory_space=pl.ANY)
    out, tables = pl.pallas_call(
        gather_kernel,
        out_shape=(
            jax.ShapeDtypeStruct((4, 2, 2, rows, 2 * width), block.dtype),
            jax.ShapeDtypeStruct((4, 2, 2) + table.shape, table.dtype),
        ),
        in_specs=[anywhere, anywhere],
        out_specs=(anywhere, anywhere),
        scratch_shapes=relay_sems(True) + relay_sems(False),
        compiler_params=params(0),
        cost_estimate=pl.CostEstimate(flops=0, bytes_accessed=100_000_000, transcendentals=0),
    )(block, table)
    tables = tables.reshape((16,) + table.shape).transpose(1, 0, 2).reshape(table.shape[0], -1)
    return out.reshape(16 * rows, 2 * width), tables


def times(left, weight, out):
    @pl.loop(0, weight.shape[1] // TILE)
    def _(j):
        span = pl.ds(pl.multiple_of(j * TILE, TILE), TILE)
        out[:, span] = jnp.dot(left[...], weight[:, span], preferred_element_type=jnp.float32)


def times_transposed(left, weight, out):
    @pl.loop(0, weight.shape[0] // TILE)
    def _(j):
        span = pl.ds(pl.multiple_of(j * TILE, TILE), TILE)
        out[:, span] = lax.dot_general(
            left[...], weight[span, :], (((1,), (1,)), ((), ())), preferred_element_type=jnp.float32
        )


def scale_of(state_f):
    return lax.rsqrt(jnp.mean(state_f * state_f, axis=-1, keepdims=True) + 1e-06)


def forward_kernel(state, levels, weight, block, xs, us, last, out, low, wide, *sems):
    relay = Relay(block, out, sems)
    enter()
    relay.start()
    last[...] = state[...]
    for step in range(3):
        xs[step] = last[...]
        state_f = last[...].astype(jnp.float32)
        low[...] = (state_f * scale_of(state_f)).astype(jnp.bfloat16)
        times(low, weight, us.at[step])
        inner = us[step]
        low[...] = (inner / (1.0 + jnp.exp(-inner))).astype(jnp.bfloat16)
        times_transposed(low, weight, wide)
        active = (levels[...] >= step + 1).astype(jnp.float32)
        last[...] = (last[...].astype(jnp.float32) + active * wide[...]).astype(jnp.bfloat16)
        relay.step(step + 1)
    relay.finish()


def forward(state, levels, weight, block):
    rows, width = state.shape
    vmem, anywhere = pl.BlockSpec(memory_space=pltpu.VMEM), pl.BlockSpec(memory_space=pl.ANY)
    xs, us, last, out = pl.pallas_call(
        forward_kernel,
        out_shape=(
            jax.ShapeDtypeStruct((3, rows, width), jnp.bfloat16),
            jax.ShapeDtypeStruct((3, rows, width), jnp.float32),
            jax.ShapeDtypeStruct((rows, width), jnp.bfloat16),
            jax.ShapeDtypeStruct((4, 2, 2) + block.shape, block.dtype),
        ),
        in_specs=[vmem, vmem, vmem, anywhere],
        out_specs=(vmem, vmem, vmem, anywhere),
        scratch_shapes=[
            pltpu.VMEM((rows, width), jnp.bfloat16),
            pltpu.VMEM((rows, width), jnp.float32),
        ]
        + relay_sems(False),
        compiler_params=params(2),
    )(state, levels, weight, block)
    return xs, us, last, out.reshape(16 * block.shape[0], block.shape[1])


def backward_kernel(
    xs, us, levels, cot, weight, block, grad, lefts, rights, out,
    full, wide, dx, lsend, lrecv, rsend, rrecv, *sems
):
    relay = Relay(block, out, sems)
    core, sibling = relay.core, relay.sibling
    half = rights.shape[3]
    mine = pl.ds(pl.multiple_of(core * half, half), half)
    theirs = pl.ds(pl.multiple_of((1 - core) * half, half), half)
    enter()
    relay.start()
    dx[...] = cot[...].astype(jnp.float32)

    def share(i):
        push(lefts.at[core, i], lefts.at[core, i], lsend.at[i], lrecv.at[i], sibling)
        rights[core, i] = full[i, :, mine]
        push(full.at[i, :, theirs], rights.at[core, i], rsend.at[i], rrecv.at[i], sibling)

    for turn, step in enumerate((2, 1, 0)):
        a, b = 2 * step, 2 * step + 1
        state_f = xs[step].astype(jnp.float32)
        rinv = scale_of(state_f)
        lefts[core, a] = (state_f * rinv).astype(jnp.bfloat16)
        active = (levels[...] >= step + 1).astype(jnp.float32)
        lefts[core, b] = (active * dx[...]).astype(jnp.bfloat16)
        times(lefts.at[core, b], weight, wide)
        inner = us[step]
        sigma = 1.0 / (1.0 + jnp.exp(-inner))
        full[b] = (inner * sigma).astype(jnp.bfloat16)
        full[a] = (wide[...] * sigma * (1.0 + inner * (1.0 - sigma))).astype(jnp.bfloat16)
        share(a)
        share(b)
        times_transposed(full.at[a], weight, wide)
        state_f = xs[step].astype(jnp.float32)
        mean = jnp.mean(wide[...] * state_f, axis=-1, keepdims=True)
        entry = dx[...] + rinv * wide[...] - state_f * (rinv * rinv * rinv * mean)
        dx[...] = entry.astype(jnp.bfloat16).astype(jnp.float32)
        relay.step(turn + 1)
    grad[...] = dx[...].astype(jnp.bfloat16)
    for i in range(6):
        landed(lefts.at[1 - core, i], lrecv.at[i])
        landed(rights.at[1 - core, i], rrecv.at[i])
        landed(lefts.at[core, i], lsend.at[i])
        landed(full.at[i, :, theirs], rsend.at[i])
    relay.finish()


def backward(xs, us, levels, cot, weight, block):
    rows, width = cot.shape
    half = weight.shape[1] // 2
    vmem, anywhere = pl.BlockSpec(memory_space=pltpu.VMEM), pl.BlockSpec(memory_space=pl.ANY)
    dma = pltpu.SemaphoreType.DMA
    grad, lefts, rights, out = pl.pallas_call(
        backward_kernel,
        out_shape=(
            jax.ShapeDtypeStruct((rows, width), jnp.bfloat16),
            jax.ShapeDtypeStruct((2, 6, rows, width), jnp.bfloat16),
            jax.ShapeDtypeStruct((2, 6, rows, half), jnp.bfloat16),
            jax.ShapeDtypeStruct((4, 2, 2) + block.shape, block.dtype),
        ),
        in_specs=[vmem] * 5 + [anywhere],
        out_specs=(vmem, vmem, vmem, anywhere),
        scratch_shapes=[
            pltpu.VMEM((6, rows, 2 * half), jnp.bfloat16),
            pltpu.VMEM((rows, width), jnp.float32),
            pltpu.VMEM((rows, width), jnp.float32),
        ]
        + [dma((6,))] * 4
        + relay_sems(False),
        compiler_params=params(3),
    )(xs, us, levels, cot, weight, block)
    merged = out.reshape(16 * block.shape[0], block.shape[1])
    return grad, lefts.reshape(-1, width), rights.reshape(-1, half), merged


def scatter_kernel(
    d, out, btake, agive, atake, total, ugive, utake, dgive, dtake,
    bsend, brecv, asend, arecv, usend, urecv, dsend, drecv,
):
    me, core = lax.axis_index("dp"), lax.axis_index("mp")
    z, y, x = place_of(me)
    half = d.shape[4] // 2
    across = ((me + 1 - 2 * x, core), (me + 2 - 4 * y, core))
    greet(z, y, x, core)
    first = 3 * (1 - z // 2)
    third = 1 + z % 2
    order = (first, 6 - first - third - z, third, z)

    def cols(h):
        return pl.ds(h * half, half)

    for zp in order:
        push(d.at[zp, 1 - y, :, :, cols(0)], btake.at[0, zp], bsend.at[0, zp], brecv.at[0, zp], across[1])
        push(d.at[zp, :, 1 - x, :, cols(1)], btake.at[1, zp], bsend.at[1, zp], brecv.at[1, zp], across[0])

    def wide(value):
        return value.astype(jnp.float32)

    def middle(zp):
        for h in range(2):
            yp, xp, far, near = (y, 1 - x, 1 - x, x) if h == 0 else (1 - y, x, 1 - y, y)
            landed(btake.at[h, zp], brecv.at[h, zp])
            agive[h, zp] = (wide(d[zp, yp, xp, :, cols(h)]) + wide(btake[h, zp, far])).astype(d.dtype)
            push(agive.at[h, zp], atake.at[h, zp], asend.at[h, zp], arecv.at[h, zp], across[h])
            total[h, zp] = wide(d[zp, y, x, :, cols(h)]) + wide(btake[h, zp, near])

    def line(zp):
        for h in range(2):
            landed(atake.at[h, zp], arecv.at[h, zp])
            total[h, zp] += wide(atake[h, zp])

            @pl.when(zp > z)
            def _():
                @pl.when(z > 0)
                def _():
                    landed(utake.at[h, zp], urecv.at[h, zp])
                    total[h, zp] += wide(utake[h, zp])

                ugive[h, zp] = total[h, zp].astype(d.dtype)
                push(ugive.at[h, zp], utake.at[h, zp], usend.at[h, zp], urecv.at[h, zp], (me + 4, core))

            @pl.when(zp < z)
            def _():
                @pl.when(z < 3)
                def _():
                    landed(dtake.at[h, zp], drecv.at[h, zp])
                    total[h, zp] += wide(dtake[h, zp])

                dgive[h, zp] = total[h, zp].astype(d.dtype)
                push(dgive.at[h, zp], dtake.at[h, zp], dsend.at[h, zp], drecv.at[h, zp], (me - 4, core))

    middle(order[0])
    for k in range(1, 4):
        middle(order[k])
        line(order[k - 1])
    line(z)
    for h in range(2):

        @pl.when(z > 0)
        def _():
            landed(utake.at[h, z], urecv.at[h, z])
            total[h, z] += wide(utake[h, z])

        @pl.when(z < 3)
        def _():
            landed(dtake.at[h, z], drecv.at[h, z])
            total[h, z] += wide(dtake[h, z])

        out[:, cols(h)] = total[h, z]
    for zp in range(4):
        for h in range(2):
            landed(btake.at[h, zp], bsend.at[h, zp])
            landed(atake.at[h, zp], asend.at[h, zp])

            @pl.when(zp > z)
            def _():
                landed(ugive.at[h, zp], usend.at[h, zp])

            @pl.when(zp < z)
            def _():
                landed(dgive.at[h, zp], dsend.at[h, zp])


def scatter_grad(partial):
    rows, width = partial.shape[0] // 16, partial.shape[1]
    half = width // 2
    dma = pltpu.SemaphoreType.DMA
    one = pltpu.VMEM((2, 4, rows, half), partial.dtype)
    return pl.pallas_call(
        scatter_kernel,
        out_shape=jax.ShapeDtypeStruct((rows, width), jnp.float32),
        in_specs=[pl.BlockSpec(memory_space=pltpu.VMEM)],
        out_specs=pl.BlockSpec(memory_space=pltpu.VMEM),
        scratch_shapes=[
            pltpu.VMEM((2, 4, 2, rows, half), partial.dtype),
            one,
            one,
            pltpu.VMEM((2, 4, rows, half), jnp.float32),
            one,
            one,
            one,
            one,
        ]
        + [dma((2, 4))] * 8,
        compiler_params=pltpu.CompilerParams(
            collective_id=1, has_side_effects=True, vmem_limit_bytes=32 * 1024 * 1024
        ),
        cost_estimate=pl.CostEstimate(flops=0, bytes_accessed=100_000_000, transcendentals=0),
    )(partial.reshape(4, 2, 2, rows, width))


def pick(table, index):
    ids = lax.broadcasted_iota(jnp.int32, (index.shape[0], table.shape[0]), 1)
    return jnp.sum(jnp.where(ids == index[:, None], table[None, :], 0), axis=1)


def find(table, value):
    ids = lax.broadcasted_iota(jnp.int32, (value.shape[0], table.shape[0]), 1)
    return jnp.sum(jnp.where(table[None, :] == value[:, None], ids, 0), axis=1)


def take_rows(index, table):
    ids = lax.broadcasted_iota(jnp.int32, (index.shape[0], table.shape[0]), 1)
    return jnp.dot(
        (ids == index[:, None]).astype(jnp.bfloat16), table, preferred_element_type=jnp.float32
    ).astype(jnp.bfloat16)


def recursions(state, levels, cot, weight):
    saved = []
    for step in range(3):
        state_f = state.astype(jnp.float32)
        rinv = lax.rsqrt(jnp.mean(state_f * state_f, axis=-1, keepdims=True) + 1e-06)
        normed = (state_f * rinv).astype(jnp.bfloat16)
        inner = jnp.dot(normed, weight, preferred_element_type=jnp.float32)
        gated = jax.nn.silu(inner).astype(jnp.bfloat16)
        branch = lax.dot_general(
            gated, weight, (((1,), (1,)), ((), ())), preferred_element_type=jnp.float32
        )
        active = (levels >= step + 1).astype(jnp.float32)[:, None]
        saved.append((state_f, rinv, normed, inner, gated, active))
        state = (state_f + active * branch).astype(jnp.bfloat16)
    final = state
    grad = cot.astype(jnp.float32)
    lefts, rights = [], []
    for step in (2, 1, 0):
        state_f, rinv, normed, inner, gated, active = saved[step]
        grad_branch = (active * grad).astype(jnp.bfloat16)
        grad_gated = jnp.dot(grad_branch, weight, preferred_element_type=jnp.float32)
        sigma = jax.nn.sigmoid(inner)
        grad_inner = (grad_gated * sigma * (1.0 + inner * (1.0 - sigma))).astype(jnp.bfloat16)
        grad_normed = lax.dot_general(
            grad_inner, weight, (((1,), (1,)), ((), ())), preferred_element_type=jnp.float32
        )
        inner_mean = jnp.mean(grad_normed * state_f, axis=-1, keepdims=True)
        entry = grad + rinv * grad_normed - state_f * rinv * rinv * rinv * inner_mean
        lefts += [normed, grad_branch]
        rights += [grad_inner, gated]
        grad = entry.astype(jnp.bfloat16).astype(jnp.float32)
    return final, grad.astype(jnp.bfloat16), jnp.concatenate(lefts), jnp.concatenate(rights)


def body(hidden_in, depth, destination, weight, cotangent):
    rows, width = hidden_in.shape
    half_inner = weight.shape[1]
    cores = lax.axis_size("mp")
    me, core = lax.axis_index("dp"), lax.axis_index("mp")
    part, strip = rows // cores, width // cores
    square = lax.axis_size("dp") == 16 and cores == 2
    state = lax.dynamic_slice_in_dim(hidden_in, core * part, part, 0)
    levels = lax.dynamic_slice_in_dim(depth, core * part, part, 0)
    cot_strip = lax.dynamic_slice_in_dim(cotangent, core * strip, strip, 1)
    if square:
        full, tables = gather_weight(weight, destination)
        high = levels.astype(jnp.float32)[:, None]
        xs, us, last, cot_all = forward(state, high, full, cot_strip)
    else:
        columns = lax.all_gather(weight, "dp", axis=0, tiled=True)
        full = lax.all_gather(columns, "mp", axis=1, tiled=True)
        tables = lax.all_gather(destination, "dp", axis=1, tiled=True)
        cot_all = lax.all_gather(cot_strip, "dp", axis=0, tiled=True)
    place = pick(tables[2], pick(tables[1], destination[0]))
    own = me * rows + jnp.arange(rows, dtype=jnp.int32)
    source = find(tables[0], find(tables[1], find(tables[2], own)))
    cot_rows = lax.all_gather(take_rows(place, cot_all), "mp", axis=1, tiled=True)
    cot = lax.dynamic_slice_in_dim(cot_rows, core * part, part, 0)
    if square:
        grad, left_all, right_half, last_all = backward(xs, us, high, cot, full, last)
    else:
        last, grad, left, right = recursions(state, levels, cot, full)
        last_all = lax.all_gather(last, "dp", axis=0, tiled=True)
        left_all = lax.all_gather(left, "mp", axis=0, tiled=True)
        right_all = lax.all_gather(right, "mp", axis=0, tiled=True)
        right_half = lax.dynamic_slice_in_dim(right_all, core * half_inner, half_inner, 1)
    owner, offset = source // rows, source % rows
    slot = jnp.where(offset // part == core, owner * part + offset % part, -1)
    final = lax.psum(take_rows(slot, last_all), "mp")
    grad_in = lax.all_gather(grad, "mp", axis=0, tiled=True)
    grad_weight = lax.dot_general(
        left_all, right_half, (((0,), (0,)), ((), ())), preferred_element_type=jnp.float32
    ).astype(jnp.bfloat16)
    if square:
        return final, grad_in, scatter_grad(grad_weight)
    owned = lax.psum_scatter(grad_weight, "dp", scatter_dimension=0, tiled=True)
    return final, grad_in, owned.astype(jnp.float32)


def solution(mesh):
    placed = (P("dp", None), P("dp"), P(None, "dp"), P("dp", "mp"), P("dp", None))
    return jax.shard_map(
        body,
        mesh=mesh,
        in_specs=placed,
        out_specs=(P("dp", None), P("dp", None), P("dp", "mp")),
        check_vma=False,
    )
```

```python
import jax
import jax.numpy as jnp
from jax import lax
from jax.experimental import pallas as pl
from jax.experimental.pallas import tpu as pltpu
from jax.sharding import PartitionSpec as P


MESH = pl.DeviceIdType.MESH
TILE = 512


def push(src, dst, send, recv, device):
    copy = pltpu.make_async_remote_copy(
        src_ref=src,
        dst_ref=dst,
        send_sem=send,
        recv_sem=recv,
        device_id=device,
        device_id_type=MESH,
    )
    copy.start()


def landed(ref, recv):
    pltpu.make_async_copy(ref, ref, recv).wait()


def place_of(me):
    return me // 4, (me // 2) % 2, me % 2


def greet(z, y, x, core):
    barrier = pltpu.get_barrier_semaphore()

    def hello(device):
        pl.semaphore_signal(barrier, inc=1, device_id=device, device_id_type=MESH)

    me = z * 4 + y * 2 + x
    hello((me, 1 - core))
    hello((me + 1 - 2 * x, core))
    hello((me + 2 - 4 * y, core))

    @pl.when(z < 3)
    def _():
        hello((me + 4, core))

    @pl.when(z > 0)
    def _():
        hello((me - 4, core))

    pl.semaphore_wait(barrier, 3 + (1 - z // 3) + (z + 2) // 3)


class Relay:
    def __init__(self, block, out, sems, paths=(0, 1), beside=False):
        self.block, self.out, self.sems, self.paths, self.beside = block, out, sems, paths, beside
        self.me, self.core = lax.axis_index("dp"), lax.axis_index("mp")
        self.z, self.y, self.x = place_of(self.me)
        self.width = block.shape[1]
        self.half = self.width // max(1, len(paths))
        self.sibling = (self.me, 1 - self.core)
        me, x, y = self.me, self.x, self.y
        self.across = ((me + 1 - 2 * x, self.core), (me + 2 - 4 * y, self.core))

    def span(self, h, core=None):
        core = self.core if core is None else core
        if not self.beside:
            return pl.ds(h * self.half, self.half)
        return pl.ds(pl.multiple_of(core * self.width + h * self.half, self.half), self.half)

    def whole(self, zp, core=None):
        core = self.core if core is None else core
        if not self.beside:
            return self.out.at[zp, self.y, self.x]
        start = pl.multiple_of(core * self.width, self.width)
        return self.out.at[zp, self.y, self.x, :, pl.ds(start, self.width)]

    def piece(self, zp, far, h, core=None):
        x, y = self.x, self.y
        if far:
            x, y = (1 - x, y) if h == 0 else (x, 1 - y)
        return self.out.at[zp, y, x, :, self.span(h, core)]

    def pair(self, zp, far, h, core=None):
        if h == 0:
            y = 1 - self.y if far else self.y
            return self.out.at[zp, y, :, :, self.span(0, core)]
        x = 1 - self.x if far else self.x
        return self.out.at[zp, :, x, :, self.span(1, core)]

    def spread(self, zp, own):
        asend, arecv = self.sems[4:6]
        for h in self.paths:
            src = self.piece(zp, False, h)
            if own:
                src = self.block.at[:, pl.ds(h * self.half, self.half)]
            push(src, self.piece(zp, False, h), asend.at[h, zp], arecv.at[h, zp], self.across[h])
        if self.beside:
            csend, crecv = self.sems[8:10]
            src = self.block if own else self.whole(zp)
            push(src, self.whole(zp), csend.at[zp], crecv.at[zp], self.sibling)

    def second(self, zp):
        arecv, bsend, brecv = self.sems[5:8]
        for h in self.paths:
            got, both = self.piece(zp, True, h), self.pair(zp, False, h)
            landed(got, arecv.at[h, zp])
            push(both, both, bsend.at[h, zp], brecv.at[h, zp], self.across[1 - h])
            if self.beside:
                cas, car = self.sems[10:12]
                push(got, got, cas.at[h, zp], car.at[h, zp], self.sibling)

    def third(self, zp):
        for h in self.paths:
            got = self.pair(zp, True, h)
            landed(got, self.sems[7].at[h, zp])
            if self.beside:
                cbs, cbr = self.sems[12:14]
                push(got, got, cbs.at[h, zp], cbr.at[h, zp], self.sibling)

    def each(self, k, act):
        z = self.z
        if k == 0:
            act(z)
            return

        @pl.when(z >= k)
        def _():
            act(z - k)

        @pl.when(z + k < 4)
        def _():
            act(z + k)

    def up(self, zp, src):
        zup, zrecv = self.sems[1], self.sems[3]

        @pl.when(self.z < 3)
        def _():
            push(src, self.whole(zp), zup.at[zp], zrecv.at[zp], (self.me + 4, self.core))

    def down(self, zp, src):
        zdn, zrecv = self.sems[2], self.sems[3]

        @pl.when(self.z > 0)
        def _():
            push(src, self.whole(zp), zdn.at[zp], zrecv.at[zp], (self.me - 4, self.core))

    def start(self):
        z = self.z
        own = pltpu.make_async_copy(self.block, self.whole(z), self.sems[0])
        own.start()
        self.up(z, self.block)
        self.down(z, self.block)
        self.spread(z, True)
        own.wait()

    def step(self, k):
        z = self.z

        @pl.when(z >= k)
        def _():
            zp = z - k
            landed(self.whole(zp), self.sems[3].at[zp])
            self.up(zp, self.whole(zp))
            self.spread(zp, False)

        @pl.when(z + k < 4)
        def _():
            zp = z + k
            landed(self.whole(zp), self.sems[3].at[zp])
            self.down(zp, self.whole(zp))
            self.spread(zp, False)

        self.each(k - 1, self.second)

    def finish(self):
        self.each(3, self.second)
        for k in range(4):
            self.each(k, self.third)
        z, other = self.z, 1 - self.core
        for zp in range(4):
            for h in self.paths:
                landed(self.piece(zp, False, h), self.sems[4].at[h, zp])
                landed(self.pair(zp, False, h), self.sems[6].at[h, zp])
            if self.beside:
                csend, crecv, cas, car, cbs, cbr = self.sems[8:14]
                landed(self.whole(zp, other), crecv.at[zp])
                landed(self.whole(zp), csend.at[zp])
                for h in self.paths:
                    landed(self.piece(zp, True, h, other), car.at[h, zp])
                    landed(self.pair(zp, True, h, other), cbr.at[h, zp])
                    landed(self.piece(zp, True, h), cas.at[h, zp])
                    landed(self.pair(zp, True, h), cbs.at[h, zp])

            @pl.when((z < 3) & (zp <= z))
            def _():
                landed(self.whole(zp), self.sems[1].at[zp])

            @pl.when((z > 0) & (zp >= z))
            def _():
                landed(self.whole(zp), self.sems[2].at[zp])


class Line(Relay):
    def __init__(self, block, out, sems):
        super().__init__(block, out, sems, paths=())

    def whole(self, zp, core=None):
        rows = self.block.shape[0]
        return self.out.at[pl.ds(zp * rows, rows)]

    def spread(self, zp, own):
        return

    def each(self, k, act):
        return


class Plane:
    def __init__(self, give, take, keep, pass_on, accept, sems):
        self.give, self.take, self.keep = give, take, keep
        self.pass_on, self.accept, self.sems = pass_on, accept, sems
        me, core = lax.axis_index("dp"), lax.axis_index("mp")
        _, self.y, self.x = place_of(me)
        self.across = ((me + 1 - 2 * self.x, core), (me + 2 - 4 * self.y, core))
        self.rows, self.half = keep.shape[2], keep.shape[3]

    def picked(self, sel, zone, yp, xp, h):
        slots = sel[pl.ds((yp * 2 + xp) * self.rows, self.rows), :]
        ids = lax.broadcasted_iota(jnp.int32, (self.rows, zone.shape[0]), 1)
        onehot = (ids == slots).astype(jnp.float32).astype(jnp.bfloat16)
        cols = zone[:, pl.ds(h * self.half, self.half)]
        return jnp.dot(onehot, cols, preferred_element_type=jnp.float32).astype(jnp.bfloat16)

    def first(self, sel, zone):
        y, x = self.y, self.x
        for h in range(2):
            for q in range(2):
                yp, xp = (q, 1 - x) if h == 0 else (1 - y, q)
                self.give[h, q] = self.picked(sel, zone, yp, xp, h)
            push(self.give.at[h], self.take.at[h], self.sems[0].at[h], self.sems[1].at[h], self.across[h])
        for h in range(2):
            for q in range(2):
                yp, xp = (q, x) if h == 0 else (y, q)
                self.keep[h, q] = self.picked(sel, zone, yp, xp, h)

    def joined(self, h, q):
        return self.keep[h, q].astype(jnp.float32) + self.take[h, q].astype(jnp.float32)

    def second(self):
        for h in range(2):
            landed(self.take.at[h], self.sems[1].at[h])
            far = 1 - self.y if h == 0 else 1 - self.x
            self.pass_on[h] = self.joined(h, far).astype(jnp.bfloat16)
            push(
                self.pass_on.at[h], self.accept.at[h], self.sems[2].at[h], self.sems[3].at[h],
                self.across[1 - h],
            )

    def third(self, strip):
        for h in range(2):
            landed(self.accept.at[h], self.sems[3].at[h])
            near = self.y if h == 0 else self.x
            value = self.joined(h, near) + self.accept[h].astype(jnp.float32)
            strip[:, pl.ds(h * self.half, self.half)] = value.astype(jnp.bfloat16)
            landed(self.give.at[h], self.sems[0].at[h])
            landed(self.pass_on.at[h], self.sems[2].at[h])


def plane_scratch(rows, half):
    two = pltpu.VMEM((2, 2, rows, half), jnp.bfloat16)
    one = pltpu.VMEM((2, rows, half), jnp.bfloat16)
    return [two, two, two, one, one] + [pltpu.SemaphoreType.DMA((2,))] * 4


def relay_sems(beside):
    dma = pltpu.SemaphoreType.DMA
    base = [dma(()), dma((4,)), dma((4,)), dma((4,))] + [dma((2, 4))] * 4
    return base + ([dma((4,)), dma((4,))] + [dma((2, 4))] * 4 if beside else [])


def enter():
    me, core = lax.axis_index("dp"), lax.axis_index("mp")
    greet(*place_of(me), core)


def gather_kernel(block, table, strip, out, tables, zone, *sems):
    main = Relay(block, out, sems[:14], beside=True)
    small = Relay(table, tables, sems[14:22], paths=(0,))
    line = Line(strip, zone, sems[22:26])
    enter()
    main.start()
    small.start()
    line.start()
    for k in range(1, 4):
        main.step(k)
        small.step(k)
        line.step(k)
    small.finish()
    main.finish()
    line.finish()


def params(number):
    return pltpu.CompilerParams(
        collective_id=number, has_side_effects=True, vmem_limit_bytes=48 * 1024 * 1024
    )


def gather_weight(block, table, strip):
    rows, width = block.shape
    anywhere = pl.BlockSpec(memory_space=pl.ANY)
    out, tables, zone = pl.pallas_call(
        gather_kernel,
        out_shape=(
            jax.ShapeDtypeStruct((4, 2, 2, rows, 2 * width), block.dtype),
            jax.ShapeDtypeStruct((4, 2, 2) + table.shape, table.dtype),
            jax.ShapeDtypeStruct((4 * strip.shape[0], strip.shape[1]), strip.dtype),
        ),
        in_specs=[anywhere] * 3,
        out_specs=(anywhere,) * 3,
        scratch_shapes=relay_sems(True) + relay_sems(False) + relay_sems(False)[:4],
        compiler_params=params(0),
        cost_estimate=pl.CostEstimate(flops=0, bytes_accessed=100_000_000, transcendentals=0),
    )(block, table, strip)
    tables = tables.reshape((16,) + table.shape).transpose(1, 0, 2).reshape(table.shape[0], -1)
    return out.reshape(16 * rows, 2 * width), tables, zone


def times(left, weight, out):
    @pl.loop(0, weight.shape[1] // TILE)
    def _(j):
        span = pl.ds(pl.multiple_of(j * TILE, TILE), TILE)
        out[:, span] = jnp.dot(left[...], weight[:, span], preferred_element_type=jnp.float32)


def times_transposed(left, weight, out):
    @pl.loop(0, weight.shape[0] // TILE)
    def _(j):
        span = pl.ds(pl.multiple_of(j * TILE, TILE), TILE)
        out[:, span] = lax.dot_general(
            left[...], weight[span, :], (((1,), (1,)), ((), ())), preferred_element_type=jnp.float32
        )


def scale_of(state_f):
    return lax.rsqrt(jnp.mean(state_f * state_f, axis=-1, keepdims=True) + 1e-06)


def recur_kernel(
    state, levels, weight, cot_zone, cot_sel, last_sel, final, grad, lefts, rights,
    xs, us, low, wide, dx, full, last, cot, cot_strip, last_strip, last_zone, end_strip, *sems
):
    cots, ends = Plane(*sems[:5], sems[5:9]), Plane(*sems[9:14], sems[14:18])
    line = Line(last_strip, last_zone, sems[18:22])
    lsend, lrecv, rsend, rrecv, esend, erecv = sems[22:]
    core, sibling = line.core, line.sibling
    part, strip, half = last.shape[0], last_strip.shape[1], rights.shape[3]
    mine = pl.ds(pl.multiple_of(core * strip, strip), strip)
    theirs = pl.ds(pl.multiple_of((1 - core) * strip, strip), strip)
    own_inner = pl.ds(pl.multiple_of(core * half, half), half)
    other_inner = pl.ds(pl.multiple_of((1 - core) * half, half), half)
    own_rows = pl.ds(pl.multiple_of(core * part, part), part)
    other_rows = pl.ds(pl.multiple_of((1 - core) * part, part), part)
    enter()
    cots.first(cot_sel, cot_zone)
    last[...] = state[...]
    for step in range(3):
        xs[step] = last[...]
        state_f = last[...].astype(jnp.float32)
        low[...] = (state_f * scale_of(state_f)).astype(jnp.bfloat16)
        times(low, weight, us.at[step])
        inner = us[step]
        low[...] = (inner / (1.0 + jnp.exp(-inner))).astype(jnp.bfloat16)
        times_transposed(low, weight, wide)
        active = (levels[...] >= step + 1).astype(jnp.float32)
        last[...] = (last[...].astype(jnp.float32) + active * wide[...]).astype(jnp.bfloat16)
        if step == 0:
            cots.second()
        if step == 1:
            cots.third(cot_strip)
            push(cot_strip.at[other_rows], cot.at[:, mine], esend.at[0], erecv.at[0], sibling)
            cot[:, mine] = cot_strip[own_rows, :]
    push(last.at[:, theirs], last_strip.at[own_rows], esend.at[1], erecv.at[1], sibling)
    last_strip[own_rows, :] = last[:, mine]
    landed(cot.at[:, theirs], erecv.at[0])
    dx[...] = cot[...].astype(jnp.float32)

    def share(i):
        push(lefts.at[core, i], lefts.at[core, i], lsend.at[i], lrecv.at[i], sibling)
        rights[core, i] = full[i, :, own_inner]
        push(full.at[i, :, other_inner], rights.at[core, i], rsend.at[i], rrecv.at[i], sibling)

    for step in (2, 1, 0):
        a, b = 2 * step, 2 * step + 1
        state_f = xs[step].astype(jnp.float32)
        rinv = scale_of(state_f)
        lefts[core, a] = (state_f * rinv).astype(jnp.bfloat16)
        active = (levels[...] >= step + 1).astype(jnp.float32)
        lefts[core, b] = (active * dx[...]).astype(jnp.bfloat16)
        times(lefts.at[core, b], weight, wide)
        if step == 2:
            landed(last_strip.at[other_rows], erecv.at[1])
            line.start()
        if step == 1:
            line.step(2)
        if step == 0:
            ends.second()
        inner = us[step]
        sigma = 1.0 / (1.0 + jnp.exp(-inner))
        full[b] = (inner * sigma).astype(jnp.bfloat16)
        full[a] = (wide[...] * sigma * (1.0 + inner * (1.0 - sigma))).astype(jnp.bfloat16)
        share(a)
        share(b)
        times_transposed(full.at[a], weight, wide)
        state_f = xs[step].astype(jnp.float32)
        mean = jnp.mean(wide[...] * state_f, axis=-1, keepdims=True)
        entry = dx[...] + rinv * wide[...] - state_f * (rinv * rinv * rinv * mean)
        dx[...] = entry.astype(jnp.bfloat16).astype(jnp.float32)
        if step == 2:
            line.step(1)
        if step == 1:
            line.step(3)
            line.finish()
            ends.first(last_sel, last_zone)
    grad[own_rows, :] = dx[...].astype(jnp.bfloat16)
    push(grad.at[own_rows], grad.at[own_rows], esend.at[2], erecv.at[2], sibling)
    ends.third(end_strip)
    push(end_strip, final.at[:, mine], esend.at[3], erecv.at[3], sibling)
    final[:, mine] = end_strip[...]
    for i in range(6):
        landed(lefts.at[1 - core, i], lrecv.at[i])
        landed(rights.at[1 - core, i], rrecv.at[i])
        landed(lefts.at[core, i], lsend.at[i])
        landed(full.at[i, :, other_inner], rsend.at[i])
    landed(cot_strip.at[other_rows], esend.at[0])
    landed(last.at[:, theirs], esend.at[1])
    landed(grad.at[own_rows], esend.at[2])
    landed(end_strip, esend.at[3])
    landed(grad.at[other_rows], erecv.at[2])
    landed(final.at[:, theirs], erecv.at[3])


def recur(state, levels, weight, cot_zone, cot_sel, last_sel):
    part, width = state.shape
    rows, half, strip = 2 * part, weight.shape[1] // 2, width // 2
    vmem = pl.BlockSpec(memory_space=pltpu.VMEM)
    dma = pltpu.SemaphoreType.DMA
    low, high = jnp.bfloat16, jnp.float32
    final, grad, lefts, rights = pl.pallas_call(
        recur_kernel,
        out_shape=(
            jax.ShapeDtypeStruct((rows, width), low),
            jax.ShapeDtypeStruct((rows, width), low),
            jax.ShapeDtypeStruct((2, 6, part, width), low),
            jax.ShapeDtypeStruct((2, 6, part, half), low),
        ),
        in_specs=[vmem] * 6,
        out_specs=(vmem,) * 4,
        scratch_shapes=[
            pltpu.VMEM((3, part, width), low),
            pltpu.VMEM((3, part, 2 * half), high),
            pltpu.VMEM((part, 2 * half), low),
            pltpu.VMEM((part, width), high),
            pltpu.VMEM((part, width), high),
            pltpu.VMEM((6, part, 2 * half), low),
            pltpu.VMEM((part, width), low),
            pltpu.VMEM((part, width), low),
            pltpu.VMEM((rows, strip), low),
            pltpu.VMEM((rows, strip), low),
            pltpu.VMEM((4 * rows, strip), low),
            pltpu.VMEM((rows, strip), low),
        ]
        + plane_scratch(rows, strip // 2) * 2
        + relay_sems(False)[:4]
        + [dma((6,))] * 4
        + [dma((4,))] * 2,
        compiler_params=params(2),
    )(state, levels, weight, cot_zone, cot_sel, last_sel)
    return final, grad, lefts.reshape(-1, width), rights.reshape(-1, half)


def scatter_kernel(
    d, out, btake, agive, atake, total, ugive, utake, dgive, dtake,
    bsend, brecv, asend, arecv, usend, urecv, dsend, drecv,
):
    me, core = lax.axis_index("dp"), lax.axis_index("mp")
    z, y, x = place_of(me)
    half = d.shape[4] // 2
    across = ((me + 1 - 2 * x, core), (me + 2 - 4 * y, core))
    greet(z, y, x, core)
    first = 3 * (1 - z // 2)
    third = 1 + z % 2
    order = (first, 6 - first - third - z, third, z)

    def cols(h):
        return pl.ds(h * half, half)

    for zp in order:
        push(d.at[zp, 1 - y, :, :, cols(0)], btake.at[0, zp], bsend.at[0, zp], brecv.at[0, zp], across[1])
        push(d.at[zp, :, 1 - x, :, cols(1)], btake.at[1, zp], bsend.at[1, zp], brecv.at[1, zp], across[0])

    def wide(value):
        return value.astype(jnp.float32)

    def middle(zp):
        for h in range(2):
            yp, xp, far, near = (y, 1 - x, 1 - x, x) if h == 0 else (1 - y, x, 1 - y, y)
            landed(btake.at[h, zp], brecv.at[h, zp])
            agive[h, zp] = (wide(d[zp, yp, xp, :, cols(h)]) + wide(btake[h, zp, far])).astype(d.dtype)
            push(agive.at[h, zp], atake.at[h, zp], asend.at[h, zp], arecv.at[h, zp], across[h])
            total[h, zp] = wide(d[zp, y, x, :, cols(h)]) + wide(btake[h, zp, near])

    def line(zp):
        for h in range(2):
            landed(atake.at[h, zp], arecv.at[h, zp])
            total[h, zp] += wide(atake[h, zp])

            @pl.when(zp > z)
            def _():
                @pl.when(z > 0)
                def _():
                    landed(utake.at[h, zp], urecv.at[h, zp])
                    total[h, zp] += wide(utake[h, zp])

                ugive[h, zp] = total[h, zp].astype(d.dtype)
                push(ugive.at[h, zp], utake.at[h, zp], usend.at[h, zp], urecv.at[h, zp], (me + 4, core))

            @pl.when(zp < z)
            def _():
                @pl.when(z < 3)
                def _():
                    landed(dtake.at[h, zp], drecv.at[h, zp])
                    total[h, zp] += wide(dtake[h, zp])

                dgive[h, zp] = total[h, zp].astype(d.dtype)
                push(dgive.at[h, zp], dtake.at[h, zp], dsend.at[h, zp], drecv.at[h, zp], (me - 4, core))

    middle(order[0])
    for k in range(1, 4):
        middle(order[k])
        line(order[k - 1])
    line(z)
    for h in range(2):

        @pl.when(z > 0)
        def _():
            landed(utake.at[h, z], urecv.at[h, z])
            total[h, z] += wide(utake[h, z])

        @pl.when(z < 3)
        def _():
            landed(dtake.at[h, z], drecv.at[h, z])
            total[h, z] += wide(dtake[h, z])

        out[:, cols(h)] = total[h, z]
    for zp in range(4):
        for h in range(2):
            landed(btake.at[h, zp], bsend.at[h, zp])
            landed(atake.at[h, zp], asend.at[h, zp])

            @pl.when(zp > z)
            def _():
                landed(ugive.at[h, zp], usend.at[h, zp])

            @pl.when(zp < z)
            def _():
                landed(dgive.at[h, zp], dsend.at[h, zp])


def scatter_grad(partial):
    rows, width = partial.shape[0] // 16, partial.shape[1]
    half = width // 2
    dma = pltpu.SemaphoreType.DMA
    one = pltpu.VMEM((2, 4, rows, half), partial.dtype)
    return pl.pallas_call(
        scatter_kernel,
        out_shape=jax.ShapeDtypeStruct((rows, width), jnp.float32),
        in_specs=[pl.BlockSpec(memory_space=pltpu.VMEM)],
        out_specs=pl.BlockSpec(memory_space=pltpu.VMEM),
        scratch_shapes=[
            pltpu.VMEM((2, 4, 2, rows, half), partial.dtype),
            one,
            one,
            pltpu.VMEM((2, 4, rows, half), jnp.float32),
            one,
            one,
            one,
            one,
        ]
        + [dma((2, 4))] * 8,
        compiler_params=pltpu.CompilerParams(
            collective_id=1, has_side_effects=True, vmem_limit_bytes=32 * 1024 * 1024
        ),
        cost_estimate=pl.CostEstimate(flops=0, bytes_accessed=100_000_000, transcendentals=0),
    )(partial.reshape(4, 2, 2, rows, width))


def pick(table, index):
    ids = lax.broadcasted_iota(jnp.int32, (index.shape[0], table.shape[0]), 1)
    return jnp.sum(jnp.where(ids == index[:, None], table[None, :], 0), axis=1)


def find(table, value):
    ids = lax.broadcasted_iota(jnp.int32, (value.shape[0], table.shape[0]), 1)
    return jnp.sum(jnp.where(table[None, :] == value[:, None], ids, 0), axis=1)


def take_rows(index, table):
    ids = lax.broadcasted_iota(jnp.int32, (index.shape[0], table.shape[0]), 1)
    return jnp.dot(
        (ids == index[:, None]).astype(jnp.bfloat16), table, preferred_element_type=jnp.float32
    ).astype(jnp.bfloat16)


def recursions(state, levels, cot, weight):
    saved = []
    for step in range(3):
        state_f = state.astype(jnp.float32)
        rinv = lax.rsqrt(jnp.mean(state_f * state_f, axis=-1, keepdims=True) + 1e-06)
        normed = (state_f * rinv).astype(jnp.bfloat16)
        inner = jnp.dot(normed, weight, preferred_element_type=jnp.float32)
        gated = jax.nn.silu(inner).astype(jnp.bfloat16)
        branch = lax.dot_general(
            gated, weight, (((1,), (1,)), ((), ())), preferred_element_type=jnp.float32
        )
        active = (levels >= step + 1).astype(jnp.float32)[:, None]
        saved.append((state_f, rinv, normed, inner, gated, active))
        state = (state_f + active * branch).astype(jnp.bfloat16)
    final = state
    grad = cot.astype(jnp.float32)
    lefts, rights = [], []
    for step in (2, 1, 0):
        state_f, rinv, normed, inner, gated, active = saved[step]
        grad_branch = (active * grad).astype(jnp.bfloat16)
        grad_gated = jnp.dot(grad_branch, weight, preferred_element_type=jnp.float32)
        sigma = jax.nn.sigmoid(inner)
        grad_inner = (grad_gated * sigma * (1.0 + inner * (1.0 - sigma))).astype(jnp.bfloat16)
        grad_normed = lax.dot_general(
            grad_inner, weight, (((1,), (1,)), ((), ())), preferred_element_type=jnp.float32
        )
        inner_mean = jnp.mean(grad_normed * state_f, axis=-1, keepdims=True)
        entry = grad + rinv * grad_normed - state_f * rinv * rinv * rinv * inner_mean
        lefts += [normed, grad_branch]
        rights += [grad_inner, gated]
        grad = entry.astype(jnp.bfloat16).astype(jnp.float32)
    return final, grad.astype(jnp.bfloat16), jnp.concatenate(lefts), jnp.concatenate(rights)


def from_column(position, rows, me):
    owner = position // rows
    return jnp.where(owner % 4 == me % 4, owner // 4 * rows + position % rows, -1)[:, None]


def body(hidden_in, depth, destination, weight, cotangent):
    rows, width = hidden_in.shape
    half_inner = weight.shape[1]
    cores = lax.axis_size("mp")
    me, core = lax.axis_index("dp"), lax.axis_index("mp")
    part, strip = rows // cores, width // cores
    state = lax.dynamic_slice_in_dim(hidden_in, core * part, part, 0)
    levels = lax.dynamic_slice_in_dim(depth, core * part, part, 0)
    cot_strip = lax.dynamic_slice_in_dim(cotangent, core * strip, strip, 1)
    contract = (((0,), (0,)), ((), ()))
    if lax.axis_size("dp") == 16 and cores == 2:
        full, tables, cot_zone = gather_weight(weight, destination, cot_strip)
        start = me // 4 * 4 * rows
        leaving = lax.dynamic_slice_in_dim(tables[0], start, 4 * rows, 0)
        place = pick(tables[2], pick(tables[1], leaving))
        own = start + jnp.arange(4 * rows, dtype=jnp.int32)
        source = find(tables[0], find(tables[1], find(tables[2], own)))
        final, grad_in, left_all, right_half = recur(
            state,
            levels.astype(jnp.float32)[:, None],
            full,
            cot_zone,
            from_column(place, rows, me),
            from_column(source, rows, me),
        )
        partial = lax.dot_general(
            left_all, right_half, contract, preferred_element_type=jnp.float32
        ).astype(jnp.bfloat16)
        return final, grad_in, scatter_grad(partial)
    columns = lax.all_gather(weight, "dp", axis=0, tiled=True)
    full = lax.all_gather(columns, "mp", axis=1, tiled=True)
    tables = lax.all_gather(destination, "dp", axis=1, tiled=True)
    cot_all = lax.all_gather(cot_strip, "dp", axis=0, tiled=True)
    place = pick(tables[2], pick(tables[1], destination[0]))
    own = me * rows + jnp.arange(rows, dtype=jnp.int32)
    source = find(tables[0], find(tables[1], find(tables[2], own)))
    cot_rows = lax.all_gather(take_rows(place, cot_all), "mp", axis=1, tiled=True)
    cot = lax.dynamic_slice_in_dim(cot_rows, core * part, part, 0)
    last, grad, left, right = recursions(state, levels, cot, full)
    last_all = lax.all_gather(last, "dp", axis=0, tiled=True)
    left_all = lax.all_gather(left, "mp", axis=0, tiled=True)
    right_all = lax.all_gather(right, "mp", axis=0, tiled=True)
    right_half = lax.dynamic_slice_in_dim(right_all, core * half_inner, half_inner, 1)
    owner, offset = source // rows, source % rows
    slot = jnp.where(offset // part == core, owner * part + offset % part, -1)
    final = lax.psum(take_rows(slot, last_all), "mp")
    grad_in = lax.all_gather(grad, "mp", axis=0, tiled=True)
    partial = lax.dot_general(
        left_all, right_half, contract, preferred_element_type=jnp.float32
    ).astype(jnp.bfloat16)
    owned = lax.psum_scatter(partial, "dp", scatter_dimension=0, tiled=True)
    return final, grad_in, owned.astype(jnp.float32)


def solution(mesh):
    placed = (P("dp", None), P("dp"), P(None, "dp"), P("dp", "mp"), P("dp", None))
    return jax.shard_map(
        body,
        mesh=mesh,
        in_specs=placed,
        out_specs=(P("dp", None), P("dp", None), P("dp", "mp")),
        check_vma=False,
    )
```

```python
import jax
import jax.numpy as jnp
from jax import lax
from jax.experimental import pallas as pl
from jax.experimental.pallas import tpu as pltpu
from jax.sharding import PartitionSpec as P


MESH = pl.DeviceIdType.MESH
TILE = 512


def push(src, dst, send, recv, device):
    copy = pltpu.make_async_remote_copy(
        src_ref=src,
        dst_ref=dst,
        send_sem=send,
        recv_sem=recv,
        device_id=device,
        device_id_type=MESH,
    )
    copy.start()


def landed(ref, recv):
    pltpu.make_async_copy(ref, ref, recv).wait()


def place_of(me):
    return me // 4, (me // 2) % 2, me % 2


def greet(z, y, x, core):
    barrier = pltpu.get_barrier_semaphore()

    def hello(device):
        pl.semaphore_signal(barrier, inc=1, device_id=device, device_id_type=MESH)

    me = z * 4 + y * 2 + x
    hello((me, 1 - core))
    hello((me + 1 - 2 * x, core))
    hello((me + 2 - 4 * y, core))

    @pl.when(z < 3)
    def _():
        hello((me + 4, core))

    @pl.when(z > 0)
    def _():
        hello((me - 4, core))

    pl.semaphore_wait(barrier, 3 + (1 - z // 3) + (z + 2) // 3)


class Relay:
    def __init__(self, block, out, sems, paths=(0, 1), beside=False):
        self.block, self.out, self.sems, self.paths, self.beside = block, out, sems, paths, beside
        self.me, self.core = lax.axis_index("dp"), lax.axis_index("mp")
        self.z, self.y, self.x = place_of(self.me)
        self.width = block.shape[1]
        self.half = self.width // max(1, len(paths))
        self.sibling = (self.me, 1 - self.core)
        me, x, y = self.me, self.x, self.y
        self.across = ((me + 1 - 2 * x, self.core), (me + 2 - 4 * y, self.core))

    def span(self, h, core=None):
        core = self.core if core is None else core
        if not self.beside:
            return pl.ds(h * self.half, self.half)
        return pl.ds(pl.multiple_of(core * self.width + h * self.half, self.half), self.half)

    def whole(self, zp, core=None):
        core = self.core if core is None else core
        if not self.beside:
            return self.out.at[zp, self.y, self.x]
        start = pl.multiple_of(core * self.width, self.width)
        return self.out.at[zp, self.y, self.x, :, pl.ds(start, self.width)]

    def piece(self, zp, far, h, core=None):
        x, y = self.x, self.y
        if far:
            x, y = (1 - x, y) if h == 0 else (x, 1 - y)
        return self.out.at[zp, y, x, :, self.span(h, core)]

    def pair(self, zp, far, h, core=None):
        if h == 0:
            y = 1 - self.y if far else self.y
            return self.out.at[zp, y, :, :, self.span(0, core)]
        x = 1 - self.x if far else self.x
        return self.out.at[zp, :, x, :, self.span(1, core)]

    def spread(self, zp, own):
        asend, arecv = self.sems[4:6]
        for h in self.paths:
            src = self.piece(zp, False, h)
            if own:
                src = self.block.at[:, pl.ds(h * self.half, self.half)]
            push(src, self.piece(zp, False, h), asend.at[h, zp], arecv.at[h, zp], self.across[h])
        if self.beside:
            csend, crecv = self.sems[8:10]
            src = self.block if own else self.whole(zp)
            push(src, self.whole(zp), csend.at[zp], crecv.at[zp], self.sibling)

    def second(self, zp):
        arecv, bsend, brecv = self.sems[5:8]
        for h in self.paths:
            got, both = self.piece(zp, True, h), self.pair(zp, False, h)
            landed(got, arecv.at[h, zp])
            push(both, both, bsend.at[h, zp], brecv.at[h, zp], self.across[1 - h])
            if self.beside:
                cas, car = self.sems[10:12]
                push(got, got, cas.at[h, zp], car.at[h, zp], self.sibling)

    def third(self, zp):
        for h in self.paths:
            got = self.pair(zp, True, h)
            landed(got, self.sems[7].at[h, zp])
            if self.beside:
                cbs, cbr = self.sems[12:14]
                push(got, got, cbs.at[h, zp], cbr.at[h, zp], self.sibling)

    def each(self, k, act):
        z = self.z
        if k == 0:
            act(z)
            return

        @pl.when(z >= k)
        def _():
            act(z - k)

        @pl.when(z + k < 4)
        def _():
            act(z + k)

    def up(self, zp, src):
        zup, zrecv = self.sems[1], self.sems[3]

        @pl.when(self.z < 3)
        def _():
            push(src, self.whole(zp), zup.at[zp], zrecv.at[zp], (self.me + 4, self.core))

    def down(self, zp, src):
        zdn, zrecv = self.sems[2], self.sems[3]

        @pl.when(self.z > 0)
        def _():
            push(src, self.whole(zp), zdn.at[zp], zrecv.at[zp], (self.me - 4, self.core))

    def start(self):
        z = self.z
        own = pltpu.make_async_copy(self.block, self.whole(z), self.sems[0])
        own.start()
        self.up(z, self.block)
        self.down(z, self.block)
        self.spread(z, True)
        own.wait()

    def step(self, k):
        z = self.z

        @pl.when(z >= k)
        def _():
            zp = z - k
            landed(self.whole(zp), self.sems[3].at[zp])
            self.up(zp, self.whole(zp))
            self.spread(zp, False)

        @pl.when(z + k < 4)
        def _():
            zp = z + k
            landed(self.whole(zp), self.sems[3].at[zp])
            self.down(zp, self.whole(zp))
            self.spread(zp, False)

        self.each(k - 1, self.second)

    def finish(self):
        z, other = self.z, 1 - self.core
        for zp in range(4):
            for h in self.paths:
                landed(self.piece(zp, False, h), self.sems[4].at[h, zp])
                landed(self.pair(zp, False, h), self.sems[6].at[h, zp])
            if self.beside:
                csend, crecv, cas, car, cbs, cbr = self.sems[8:14]
                landed(self.whole(zp, other), crecv.at[zp])
                landed(self.whole(zp), csend.at[zp])
                for h in self.paths:
                    landed(self.piece(zp, True, h, other), car.at[h, zp])
                    landed(self.pair(zp, True, h, other), cbr.at[h, zp])
                    landed(self.piece(zp, True, h), cas.at[h, zp])
                    landed(self.pair(zp, True, h), cbs.at[h, zp])

            @pl.when((z < 3) & (zp <= z))
            def _():
                landed(self.whole(zp), self.sems[1].at[zp])

            @pl.when((z > 0) & (zp >= z))
            def _():
                landed(self.whole(zp), self.sems[2].at[zp])


class Line(Relay):
    def __init__(self, block, out, sems):
        super().__init__(block, out, sems, paths=())

    def whole(self, zp, core=None):
        rows = self.block.shape[0]
        return self.out.at[pl.ds(zp * rows, rows)]

    def spread(self, zp, own):
        return

    def each(self, k, act):
        return


class Plane:
    def __init__(self, give, take, keep, pass_on, accept, sems):
        self.give, self.take, self.keep = give, take, keep
        self.pass_on, self.accept, self.sems = pass_on, accept, sems
        me, core = lax.axis_index("dp"), lax.axis_index("mp")
        _, self.y, self.x = place_of(me)
        self.across = ((me + 1 - 2 * self.x, core), (me + 2 - 4 * self.y, core))
        self.rows, self.half = keep.shape[2], keep.shape[3]

    def picked(self, sel, zone, yp, xp, h):
        slots = sel[pl.ds((yp * 2 + xp) * self.rows, self.rows), :]
        ids = lax.broadcasted_iota(jnp.int32, (self.rows, zone.shape[0]), 1)
        onehot = (ids == slots).astype(jnp.float32).astype(jnp.bfloat16)
        cols = zone[:, pl.ds(h * self.half, self.half)]
        return jnp.dot(onehot, cols, preferred_element_type=jnp.float32).astype(jnp.bfloat16)

    def first(self, sel, zone):
        y, x = self.y, self.x
        for h in range(2):
            for q in range(2):
                yp, xp = (q, 1 - x) if h == 0 else (1 - y, q)
                self.give[h, q] = self.picked(sel, zone, yp, xp, h)
            push(self.give.at[h], self.take.at[h], self.sems[0].at[h], self.sems[1].at[h], self.across[h])
        for h in range(2):
            for q in range(2):
                yp, xp = (q, x) if h == 0 else (y, q)
                self.keep[h, q] = self.picked(sel, zone, yp, xp, h)

    def joined(self, h, q):
        return self.keep[h, q].astype(jnp.float32) + self.take[h, q].astype(jnp.float32)

    def second(self):
        for h in range(2):
            landed(self.take.at[h], self.sems[1].at[h])
            far = 1 - self.y if h == 0 else 1 - self.x
            self.pass_on[h] = self.joined(h, far).astype(jnp.bfloat16)
            push(
                self.pass_on.at[h], self.accept.at[h], self.sems[2].at[h], self.sems[3].at[h],
                self.across[1 - h],
            )

    def third(self, strip):
        for h in range(2):
            landed(self.accept.at[h], self.sems[3].at[h])
            near = self.y if h == 0 else self.x
            value = self.joined(h, near) + self.accept[h].astype(jnp.float32)
            strip[:, pl.ds(h * self.half, self.half)] = value.astype(jnp.bfloat16)
            landed(self.give.at[h], self.sems[0].at[h])
            landed(self.pass_on.at[h], self.sems[2].at[h])


def plane_scratch(rows, half):
    two = pltpu.VMEM((2, 2, rows, half), jnp.bfloat16)
    one = pltpu.VMEM((2, rows, half), jnp.bfloat16)
    return [two, two, two, one, one] + [pltpu.SemaphoreType.DMA((2,))] * 4


def relay_sems(beside):
    dma = pltpu.SemaphoreType.DMA
    base = [dma(()), dma((4,)), dma((4,)), dma((4,))] + [dma((2, 4))] * 4
    return base + ([dma((4,)), dma((4,))] + [dma((2, 4))] * 4 if beside else [])


def enter():
    me, core = lax.axis_index("dp"), lax.axis_index("mp")
    greet(*place_of(me), core)


def gather_kernel(block, table, strip, out, tables, zone, *sems):
    main = Relay(block, out, sems[:14], beside=True)
    small = Relay(table, tables, sems[14:22], paths=(0,))
    line = Line(strip, zone, sems[22:26])
    enter()
    main.start()
    small.start()
    for k in range(1, 4):
        main.step(k)
        small.step(k)
    line.start()
    main.each(3, main.second)
    line.step(1)
    small.each(3, small.second)
    for k in range(4):
        small.each(k, small.third)
    small.finish()
    for k in range(4):
        main.each(k, main.third)
        if k in (0, 2):
            line.step(2 + k // 2)
    main.finish()
    line.finish()


def params(number):
    return pltpu.CompilerParams(
        collective_id=number, has_side_effects=True, vmem_limit_bytes=48 * 1024 * 1024
    )


def gather_weight(block, table, strip):
    rows, width = block.shape
    anywhere = pl.BlockSpec(memory_space=pl.ANY)
    out, tables, zone = pl.pallas_call(
        gather_kernel,
        out_shape=(
            jax.ShapeDtypeStruct((4, 2, 2, rows, 2 * width), block.dtype),
            jax.ShapeDtypeStruct((4, 2, 2) + table.shape, table.dtype),
            jax.ShapeDtypeStruct((4 * strip.shape[0], strip.shape[1]), strip.dtype),
        ),
        in_specs=[anywhere] * 3,
        out_specs=(anywhere,) * 3,
        scratch_shapes=relay_sems(True) + relay_sems(False) + relay_sems(False)[:4],
        compiler_params=params(0),
        cost_estimate=pl.CostEstimate(flops=0, bytes_accessed=100_000_000, transcendentals=0),
    )(block, table, strip)
    tables = tables.reshape((16,) + table.shape).transpose(1, 0, 2).reshape(table.shape[0], -1)
    return out.reshape(16 * rows, 2 * width), tables, zone


def times(left, weight, out):
    @pl.loop(0, weight.shape[1] // TILE)
    def _(j):
        span = pl.ds(pl.multiple_of(j * TILE, TILE), TILE)
        out[:, span] = jnp.dot(left[...], weight[:, span], preferred_element_type=jnp.float32)


def times_transposed(left, weight, out):
    @pl.loop(0, weight.shape[0] // TILE)
    def _(j):
        span = pl.ds(pl.multiple_of(j * TILE, TILE), TILE)
        out[:, span] = lax.dot_general(
            left[...], weight[span, :], (((1,), (1,)), ((), ())), preferred_element_type=jnp.float32
        )


def scale_of(state_f):
    return lax.rsqrt(jnp.mean(state_f * state_f, axis=-1, keepdims=True) + 1e-06)


def recur_kernel(
    state, levels, weight, cot_zone, cot_sel, last_sel, final, grad, lefts, rights,
    xs, us, low, wide, dx, full, last, cot, cot_strip, last_strip, last_zone, end_strip, *sems
):
    cots, ends = Plane(*sems[:5], sems[5:9]), Plane(*sems[9:14], sems[14:18])
    line = Line(last_strip, last_zone, sems[18:22])
    lsend, lrecv, rsend, rrecv, esend, erecv = sems[22:]
    core, sibling = line.core, line.sibling
    part, strip, half = last.shape[0], last_strip.shape[1], rights.shape[3]
    mine = pl.ds(pl.multiple_of(core * strip, strip), strip)
    theirs = pl.ds(pl.multiple_of((1 - core) * strip, strip), strip)
    own_inner = pl.ds(pl.multiple_of(core * half, half), half)
    other_inner = pl.ds(pl.multiple_of((1 - core) * half, half), half)
    own_rows = pl.ds(pl.multiple_of(core * part, part), part)
    other_rows = pl.ds(pl.multiple_of((1 - core) * part, part), part)
    enter()
    cots.first(cot_sel, cot_zone)
    last[...] = state[...]
    for step in range(3):
        xs[step] = last[...]
        state_f = last[...].astype(jnp.float32)
        low[...] = (state_f * scale_of(state_f)).astype(jnp.bfloat16)
        times(low, weight, us.at[step])
        inner = us[step]
        low[...] = (inner / (1.0 + jnp.exp(-inner))).astype(jnp.bfloat16)
        times_transposed(low, weight, wide)
        active = (levels[...] >= step + 1).astype(jnp.float32)
        last[...] = (last[...].astype(jnp.float32) + active * wide[...]).astype(jnp.bfloat16)
        if step == 0:
            cots.second()
        if step == 1:
            cots.third(cot_strip)
            push(cot_strip.at[other_rows], cot.at[:, mine], esend.at[0], erecv.at[0], sibling)
            cot[:, mine] = cot_strip[own_rows, :]
    push(last.at[:, theirs], last_strip.at[own_rows], esend.at[1], erecv.at[1], sibling)
    last_strip[own_rows, :] = last[:, mine]
    landed(cot.at[:, theirs], erecv.at[0])
    dx[...] = cot[...].astype(jnp.float32)

    def share(i):
        push(lefts.at[core, i], lefts.at[core, i], lsend.at[i], lrecv.at[i], sibling)
        rights[core, i] = full[i, :, own_inner]
        push(full.at[i, :, other_inner], rights.at[core, i], rsend.at[i], rrecv.at[i], sibling)

    for step in (2, 1, 0):
        a, b = 2 * step, 2 * step + 1
        state_f = xs[step].astype(jnp.float32)
        rinv = scale_of(state_f)
        lefts[core, a] = (state_f * rinv).astype(jnp.bfloat16)
        active = (levels[...] >= step + 1).astype(jnp.float32)
        lefts[core, b] = (active * dx[...]).astype(jnp.bfloat16)
        times(lefts.at[core, b], weight, wide)
        if step == 2:
            landed(last_strip.at[other_rows], erecv.at[1])
            line.start()
        if step == 1:
            line.step(2)
        if step == 0:
            ends.second()
        inner = us[step]
        sigma = 1.0 / (1.0 + jnp.exp(-inner))
        full[b] = (inner * sigma).astype(jnp.bfloat16)
        full[a] = (wide[...] * sigma * (1.0 + inner * (1.0 - sigma))).astype(jnp.bfloat16)
        share(a)
        share(b)
        times_transposed(full.at[a], weight, wide)
        state_f = xs[step].astype(jnp.float32)
        mean = jnp.mean(wide[...] * state_f, axis=-1, keepdims=True)
        entry = dx[...] + rinv * wide[...] - state_f * (rinv * rinv * rinv * mean)
        dx[...] = entry.astype(jnp.bfloat16).astype(jnp.float32)
        if step == 2:
            line.step(1)
        if step == 1:
            line.step(3)
            line.finish()
            ends.first(last_sel, last_zone)
    grad[own_rows, :] = dx[...].astype(jnp.bfloat16)
    push(grad.at[own_rows], grad.at[own_rows], esend.at[2], erecv.at[2], sibling)
    ends.third(end_strip)
    push(end_strip, final.at[:, mine], esend.at[3], erecv.at[3], sibling)
    final[:, mine] = end_strip[...]
    for i in range(6):
        landed(lefts.at[1 - core, i], lrecv.at[i])
        landed(rights.at[1 - core, i], rrecv.at[i])
        landed(lefts.at[core, i], lsend.at[i])
        landed(full.at[i, :, other_inner], rsend.at[i])
    landed(cot_strip.at[other_rows], esend.at[0])
    landed(last.at[:, theirs], esend.at[1])
    landed(grad.at[own_rows], esend.at[2])
    landed(end_strip, esend.at[3])
    landed(grad.at[other_rows], erecv.at[2])
    landed(final.at[:, theirs], erecv.at[3])


def recur(state, levels, weight, cot_zone, cot_sel, last_sel):
    part, width = state.shape
    rows, half, strip = 2 * part, weight.shape[1] // 2, width // 2
    vmem = pl.BlockSpec(memory_space=pltpu.VMEM)
    dma = pltpu.SemaphoreType.DMA
    low, high = jnp.bfloat16, jnp.float32
    final, grad, lefts, rights = pl.pallas_call(
        recur_kernel,
        out_shape=(
            jax.ShapeDtypeStruct((rows, width), low),
            jax.ShapeDtypeStruct((rows, width), low),
            jax.ShapeDtypeStruct((2, 6, part, width), low),
            jax.ShapeDtypeStruct((2, 6, part, half), low),
        ),
        in_specs=[vmem] * 6,
        out_specs=(vmem,) * 4,
        scratch_shapes=[
            pltpu.VMEM((3, part, width), low),
            pltpu.VMEM((3, part, 2 * half), high),
            pltpu.VMEM((part, 2 * half), low),
            pltpu.VMEM((part, width), high),
            pltpu.VMEM((part, width), high),
            pltpu.VMEM((6, part, 2 * half), low),
            pltpu.VMEM((part, width), low),
            pltpu.VMEM((part, width), low),
            pltpu.VMEM((rows, strip), low),
            pltpu.VMEM((rows, strip), low),
            pltpu.VMEM((4 * rows, strip), low),
            pltpu.VMEM((rows, strip), low),
        ]
        + plane_scratch(rows, strip // 2) * 2
        + relay_sems(False)[:4]
        + [dma((6,))] * 4
        + [dma((4,))] * 2,
        compiler_params=params(2),
    )(state, levels, weight, cot_zone, cot_sel, last_sel)
    return final, grad, lefts.reshape(-1, width), rights.reshape(-1, half)


def scatter_kernel(
    left, right, out, d, btake, agive, atake, total, ugive, utake, dgive, dtake,
    bsend, brecv, asend, arecv, usend, urecv, dsend, drecv,
):
    me, core = lax.axis_index("dp"), lax.axis_index("mp")
    z, y, x = place_of(me)
    half = d.shape[4] // 2
    group = left.shape[1] // 4
    across = ((me + 1 - 2 * x, core), (me + 2 - 4 * y, core))
    greet(z, y, x, core)
    first = 3 * (1 - z // 2)
    third = 1 + z % 2
    order = (first, 6 - first - third - z, third, z)

    def cols(h):
        return pl.ds(h * half, half)

    for zp in order:
        span = pl.ds(pl.multiple_of(zp * group, group), group)
        product = lax.dot_general(
            left[:, span], right[...], (((0,), (0,)), ((), ())), preferred_element_type=jnp.float32
        )
        d[zp] = product.astype(d.dtype).reshape(d.shape[1:])
        push(d.at[zp, 1 - y, :, :, cols(0)], btake.at[0, zp], bsend.at[0, zp], brecv.at[0, zp], across[1])
        push(d.at[zp, :, 1 - x, :, cols(1)], btake.at[1, zp], bsend.at[1, zp], brecv.at[1, zp], across[0])

    def wide(value):
        return value.astype(jnp.float32)

    def middle(zp):
        for h in range(2):
            yp, xp, far, near = (y, 1 - x, 1 - x, x) if h == 0 else (1 - y, x, 1 - y, y)
            landed(btake.at[h, zp], brecv.at[h, zp])
            agive[h, zp] = (wide(d[zp, yp, xp, :, cols(h)]) + wide(btake[h, zp, far])).astype(d.dtype)
            push(agive.at[h, zp], atake.at[h, zp], asend.at[h, zp], arecv.at[h, zp], across[h])
            total[h, zp] = wide(d[zp, y, x, :, cols(h)]) + wide(btake[h, zp, near])

    def line(zp):
        for h in range(2):
            landed(atake.at[h, zp], arecv.at[h, zp])
            total[h, zp] += wide(atake[h, zp])

            @pl.when(zp > z)
            def _():
                @pl.when(z > 0)
                def _():
                    landed(utake.at[h, zp], urecv.at[h, zp])
                    total[h, zp] += wide(utake[h, zp])

                ugive[h, zp] = total[h, zp].astype(d.dtype)
                push(ugive.at[h, zp], utake.at[h, zp], usend.at[h, zp], urecv.at[h, zp], (me + 4, core))

            @pl.when(zp < z)
            def _():
                @pl.when(z < 3)
                def _():
                    landed(dtake.at[h, zp], drecv.at[h, zp])
                    total[h, zp] += wide(dtake[h, zp])

                dgive[h, zp] = total[h, zp].astype(d.dtype)
                push(dgive.at[h, zp], dtake.at[h, zp], dsend.at[h, zp], drecv.at[h, zp], (me - 4, core))

    middle(order[0])
    for k in range(1, 4):
        middle(order[k])
        line(order[k - 1])
    line(z)
    for h in range(2):

        @pl.when(z > 0)
        def _():
            landed(utake.at[h, z], urecv.at[h, z])
            total[h, z] += wide(utake[h, z])

        @pl.when(z < 3)
        def _():
            landed(dtake.at[h, z], drecv.at[h, z])
            total[h, z] += wide(dtake[h, z])

        out[:, cols(h)] = total[h, z]
    for zp in range(4):
        for h in range(2):
            landed(btake.at[h, zp], bsend.at[h, zp])
            landed(atake.at[h, zp], asend.at[h, zp])

            @pl.when(zp > z)
            def _():
                landed(ugive.at[h, zp], usend.at[h, zp])

            @pl.when(zp < z)
            def _():
                landed(dgive.at[h, zp], dsend.at[h, zp])


def scatter_grad(left, right):
    rows, width = left.shape[1] // 16, right.shape[1]
    half = width // 2
    dma = pltpu.SemaphoreType.DMA
    one = pltpu.VMEM((2, 4, rows, half), left.dtype)
    return pl.pallas_call(
        scatter_kernel,
        out_shape=jax.ShapeDtypeStruct((rows, width), jnp.float32),
        in_specs=[pl.BlockSpec(memory_space=pltpu.VMEM)] * 2,
        out_specs=pl.BlockSpec(memory_space=pltpu.VMEM),
        scratch_shapes=[
            pltpu.VMEM((4, 2, 2, rows, width), left.dtype),
            pltpu.VMEM((2, 4, 2, rows, half), left.dtype),
            one,
            one,
            pltpu.VMEM((2, 4, rows, half), jnp.float32),
            one,
            one,
            one,
            one,
        ]
        + [dma((2, 4))] * 8,
        compiler_params=pltpu.CompilerParams(
            collective_id=1, has_side_effects=True, vmem_limit_bytes=32 * 1024 * 1024
        ),
        cost_estimate=pl.CostEstimate(flops=0, bytes_accessed=100_000_000, transcendentals=0),
    )(left, right)


def pick(table, index):
    ids = lax.broadcasted_iota(jnp.int32, (index.shape[0], table.shape[0]), 1)
    return jnp.sum(jnp.where(ids == index[:, None], table[None, :], 0), axis=1)


def find(table, value):
    ids = lax.broadcasted_iota(jnp.int32, (value.shape[0], table.shape[0]), 1)
    return jnp.sum(jnp.where(table[None, :] == value[:, None], ids, 0), axis=1)


def take_rows(index, table):
    ids = lax.broadcasted_iota(jnp.int32, (index.shape[0], table.shape[0]), 1)
    return jnp.dot(
        (ids == index[:, None]).astype(jnp.bfloat16), table, preferred_element_type=jnp.float32
    ).astype(jnp.bfloat16)


def recursions(state, levels, cot, weight):
    saved = []
    for step in range(3):
        state_f = state.astype(jnp.float32)
        rinv = lax.rsqrt(jnp.mean(state_f * state_f, axis=-1, keepdims=True) + 1e-06)
        normed = (state_f * rinv).astype(jnp.bfloat16)
        inner = jnp.dot(normed, weight, preferred_element_type=jnp.float32)
        gated = jax.nn.silu(inner).astype(jnp.bfloat16)
        branch = lax.dot_general(
            gated, weight, (((1,), (1,)), ((), ())), preferred_element_type=jnp.float32
        )
        active = (levels >= step + 1).astype(jnp.float32)[:, None]
        saved.append((state_f, rinv, normed, inner, gated, active))
        state = (state_f + active * branch).astype(jnp.bfloat16)
    final = state
    grad = cot.astype(jnp.float32)
    lefts, rights = [], []
    for step in (2, 1, 0):
        state_f, rinv, normed, inner, gated, active = saved[step]
        grad_branch = (active * grad).astype(jnp.bfloat16)
        grad_gated = jnp.dot(grad_branch, weight, preferred_element_type=jnp.float32)
        sigma = jax.nn.sigmoid(inner)
        grad_inner = (grad_gated * sigma * (1.0 + inner * (1.0 - sigma))).astype(jnp.bfloat16)
        grad_normed = lax.dot_general(
            grad_inner, weight, (((1,), (1,)), ((), ())), preferred_element_type=jnp.float32
        )
        inner_mean = jnp.mean(grad_normed * state_f, axis=-1, keepdims=True)
        entry = grad + rinv * grad_normed - state_f * rinv * rinv * rinv * inner_mean
        lefts += [normed, grad_branch]
        rights += [grad_inner, gated]
        grad = entry.astype(jnp.bfloat16).astype(jnp.float32)
    return final, grad.astype(jnp.bfloat16), jnp.concatenate(lefts), jnp.concatenate(rights)


def from_column(position, rows, me):
    owner = position // rows
    return jnp.where(owner % 4 == me % 4, owner // 4 * rows + position % rows, -1)[:, None]


def body(hidden_in, depth, destination, weight, cotangent):
    rows, width = hidden_in.shape
    half_inner = weight.shape[1]
    cores = lax.axis_size("mp")
    me, core = lax.axis_index("dp"), lax.axis_index("mp")
    part, strip = rows // cores, width // cores
    state = lax.dynamic_slice_in_dim(hidden_in, core * part, part, 0)
    levels = lax.dynamic_slice_in_dim(depth, core * part, part, 0)
    cot_strip = lax.dynamic_slice_in_dim(cotangent, core * strip, strip, 1)
    contract = (((0,), (0,)), ((), ()))
    if lax.axis_size("dp") == 16 and cores == 2:
        full, tables, cot_zone = gather_weight(weight, destination, cot_strip)
        start = me // 4 * 4 * rows
        leaving = lax.dynamic_slice_in_dim(tables[0], start, 4 * rows, 0)
        place = pick(tables[2], pick(tables[1], leaving))
        own = start + jnp.arange(4 * rows, dtype=jnp.int32)
        source = find(tables[0], find(tables[1], find(tables[2], own)))
        final, grad_in, left_all, right_half = recur(
            state,
            levels.astype(jnp.float32)[:, None],
            full,
            cot_zone,
            from_column(place, rows, me),
            from_column(source, rows, me),
        )
        return final, grad_in, scatter_grad(left_all, right_half)
    columns = lax.all_gather(weight, "dp", axis=0, tiled=True)
    full = lax.all_gather(columns, "mp", axis=1, tiled=True)
    tables = lax.all_gather(destination, "dp", axis=1, tiled=True)
    cot_all = lax.all_gather(cot_strip, "dp", axis=0, tiled=True)
    place = pick(tables[2], pick(tables[1], destination[0]))
    own = me * rows + jnp.arange(rows, dtype=jnp.int32)
    source = find(tables[0], find(tables[1], find(tables[2], own)))
    cot_rows = lax.all_gather(take_rows(place, cot_all), "mp", axis=1, tiled=True)
    cot = lax.dynamic_slice_in_dim(cot_rows, core * part, part, 0)
    last, grad, left, right = recursions(state, levels, cot, full)
    last_all = lax.all_gather(last, "dp", axis=0, tiled=True)
    left_all = lax.all_gather(left, "mp", axis=0, tiled=True)
    right_all = lax.all_gather(right, "mp", axis=0, tiled=True)
    right_half = lax.dynamic_slice_in_dim(right_all, core * half_inner, half_inner, 1)
    owner, offset = source // rows, source % rows
    slot = jnp.where(offset // part == core, owner * part + offset % part, -1)
    final = lax.psum(take_rows(slot, last_all), "mp")
    grad_in = lax.all_gather(grad, "mp", axis=0, tiled=True)
    partial = lax.dot_general(
        left_all, right_half, contract, preferred_element_type=jnp.float32
    ).astype(jnp.bfloat16)
    owned = lax.psum_scatter(partial, "dp", scatter_dimension=0, tiled=True)
    return final, grad_in, owned.astype(jnp.float32)


def solution(mesh):
    placed = (P("dp", None), P("dp"), P(None, "dp"), P("dp", "mp"), P("dp", None))
    return jax.shard_map(
        body,
        mesh=mesh,
        in_specs=placed,
        out_specs=(P("dp", None), P("dp", None), P("dp", "mp")),
        check_vma=False,
    )
```

```python
import jax
import jax.numpy as jnp
from jax import lax
from jax.experimental import pallas as pl
from jax.experimental.pallas import tpu as pltpu
from jax.sharding import PartitionSpec as P


MESH = pl.DeviceIdType.MESH
TILE = 512


def push(src, dst, send, recv, device):
    copy = pltpu.make_async_remote_copy(
        src_ref=src,
        dst_ref=dst,
        send_sem=send,
        recv_sem=recv,
        device_id=device,
        device_id_type=MESH,
    )
    copy.start()


def landed(ref, recv):
    pltpu.make_async_copy(ref, ref, recv).wait()


def place_of(me):
    return me // 4, (me // 2) % 2, me % 2


def greet(z, y, x, core):
    barrier = pltpu.get_barrier_semaphore()

    def hello(device):
        pl.semaphore_signal(barrier, inc=1, device_id=device, device_id_type=MESH)

    me = z * 4 + y * 2 + x
    hello((me, 1 - core))
    hello((me + 1 - 2 * x, core))
    hello((me + 2 - 4 * y, core))

    @pl.when(z < 3)
    def _():
        hello((me + 4, core))

    @pl.when(z > 0)
    def _():
        hello((me - 4, core))

    pl.semaphore_wait(barrier, 3 + (1 - z // 3) + (z + 2) // 3)


class Relay:
    def __init__(self, block, out, sems, paths=(0, 1), beside=False):
        self.block, self.out, self.sems, self.paths, self.beside = block, out, sems, paths, beside
        self.me, self.core = lax.axis_index("dp"), lax.axis_index("mp")
        self.z, self.y, self.x = place_of(self.me)
        self.width = block.shape[1]
        self.half = self.width // max(1, len(paths))
        self.sibling = (self.me, 1 - self.core)
        me, x, y = self.me, self.x, self.y
        self.across = ((me + 1 - 2 * x, self.core), (me + 2 - 4 * y, self.core))

    def span(self, h, core=None):
        core = self.core if core is None else core
        if not self.beside:
            return pl.ds(h * self.half, self.half)
        return pl.ds(pl.multiple_of(core * self.width + h * self.half, self.half), self.half)

    def whole(self, zp, core=None):
        core = self.core if core is None else core
        if not self.beside:
            return self.out.at[zp, self.y, self.x]
        start = pl.multiple_of(core * self.width, self.width)
        return self.out.at[zp, self.y, self.x, :, pl.ds(start, self.width)]

    def piece(self, zp, far, h, core=None):
        x, y = self.x, self.y
        if far:
            x, y = (1 - x, y) if h == 0 else (x, 1 - y)
        return self.out.at[zp, y, x, :, self.span(h, core)]

    def pair(self, zp, far, h, core=None):
        if h == 0:
            y = 1 - self.y if far else self.y
            return self.out.at[zp, y, :, :, self.span(0, core)]
        x = 1 - self.x if far else self.x
        return self.out.at[zp, :, x, :, self.span(1, core)]

    def spread(self, zp, own):
        asend, arecv = self.sems[4:6]
        for h in self.paths:
            src = self.piece(zp, False, h)
            if own:
                src = self.block.at[:, pl.ds(h * self.half, self.half)]
            push(src, self.piece(zp, False, h), asend.at[h, zp], arecv.at[h, zp], self.across[h])
        if self.beside:
            csend, crecv = self.sems[8:10]
            src = self.block if own else self.whole(zp)
            push(src, self.whole(zp), csend.at[zp], crecv.at[zp], self.sibling)

    def second(self, zp):
        arecv, bsend, brecv = self.sems[5:8]
        for h in self.paths:
            got, both = self.piece(zp, True, h), self.pair(zp, False, h)
            landed(got, arecv.at[h, zp])
            push(both, both, bsend.at[h, zp], brecv.at[h, zp], self.across[1 - h])
            if self.beside:
                cas, car = self.sems[10:12]
                push(got, got, cas.at[h, zp], car.at[h, zp], self.sibling)

    def third(self, zp):
        for h in self.paths:
            got = self.pair(zp, True, h)
            landed(got, self.sems[7].at[h, zp])
            if self.beside:
                cbs, cbr = self.sems[12:14]
                push(got, got, cbs.at[h, zp], cbr.at[h, zp], self.sibling)

    def each(self, k, act):
        z = self.z
        if k == 0:
            act(z)
            return

        @pl.when(z >= k)
        def _():
            act(z - k)

        @pl.when(z + k < 4)
        def _():
            act(z + k)

    def up(self, zp, src):
        zup, zrecv = self.sems[1], self.sems[3]

        @pl.when(self.z < 3)
        def _():
            push(src, self.whole(zp), zup.at[zp], zrecv.at[zp], (self.me + 4, self.core))

    def down(self, zp, src):
        zdn, zrecv = self.sems[2], self.sems[3]

        @pl.when(self.z > 0)
        def _():
            push(src, self.whole(zp), zdn.at[zp], zrecv.at[zp], (self.me - 4, self.core))

    def start(self):
        z = self.z
        own = pltpu.make_async_copy(self.block, self.whole(z), self.sems[0])
        own.start()
        self.up(z, self.block)
        self.down(z, self.block)
        self.spread(z, True)
        own.wait()

    def step(self, k):
        z = self.z

        @pl.when(z >= k)
        def _():
            zp = z - k
            landed(self.whole(zp), self.sems[3].at[zp])
            self.up(zp, self.whole(zp))
            self.spread(zp, False)

        @pl.when(z + k < 4)
        def _():
            zp = z + k
            landed(self.whole(zp), self.sems[3].at[zp])
            self.down(zp, self.whole(zp))
            self.spread(zp, False)

        self.each(k - 1, self.second)

    def finish(self):
        z, other = self.z, 1 - self.core
        for zp in range(4):
            for h in self.paths:
                landed(self.piece(zp, False, h), self.sems[4].at[h, zp])
                landed(self.pair(zp, False, h), self.sems[6].at[h, zp])
            if self.beside:
                csend, crecv, cas, car, cbs, cbr = self.sems[8:14]
                landed(self.whole(zp, other), crecv.at[zp])
                landed(self.whole(zp), csend.at[zp])
                for h in self.paths:
                    landed(self.piece(zp, True, h, other), car.at[h, zp])
                    landed(self.pair(zp, True, h, other), cbr.at[h, zp])
                    landed(self.piece(zp, True, h), cas.at[h, zp])
                    landed(self.pair(zp, True, h), cbs.at[h, zp])

            @pl.when((z < 3) & (zp <= z))
            def _():
                landed(self.whole(zp), self.sems[1].at[zp])

            @pl.when((z > 0) & (zp >= z))
            def _():
                landed(self.whole(zp), self.sems[2].at[zp])


class Line(Relay):
    def __init__(self, block, out, sems):
        super().__init__(block, out, sems, paths=())

    def whole(self, zp, core=None):
        rows = self.block.shape[0]
        return self.out.at[pl.ds(zp * rows, rows)]

    def spread(self, zp, own):
        return

    def each(self, k, act):
        return


class Plane:
    def __init__(self, give, take, keep, pass_on, accept, sems):
        self.give, self.take, self.keep = give, take, keep
        self.pass_on, self.accept, self.sems = pass_on, accept, sems
        me, core = lax.axis_index("dp"), lax.axis_index("mp")
        _, self.y, self.x = place_of(me)
        self.across = ((me + 1 - 2 * self.x, core), (me + 2 - 4 * self.y, core))
        self.rows, self.half = keep.shape[2], keep.shape[3]

    def picked(self, sel, zone, yp, xp, h):
        slots = sel[pl.ds((yp * 2 + xp) * self.rows, self.rows), :]
        ids = lax.broadcasted_iota(jnp.int32, (self.rows, zone.shape[0]), 1)
        onehot = (ids == slots).astype(jnp.float32).astype(jnp.bfloat16)
        cols = zone[:, pl.ds(h * self.half, self.half)]
        return jnp.dot(onehot, cols, preferred_element_type=jnp.float32).astype(jnp.bfloat16)

    def first(self, sel, zone):
        y, x = self.y, self.x
        for h in range(2):
            for q in range(2):
                yp, xp = (q, 1 - x) if h == 0 else (1 - y, q)
                self.give[h, q] = self.picked(sel, zone, yp, xp, h)
            push(self.give.at[h], self.take.at[h], self.sems[0].at[h], self.sems[1].at[h], self.across[h])
        for h in range(2):
            for q in range(2):
                yp, xp = (q, x) if h == 0 else (y, q)
                self.keep[h, q] = self.picked(sel, zone, yp, xp, h)

    def joined(self, h, q):
        return self.keep[h, q].astype(jnp.float32) + self.take[h, q].astype(jnp.float32)

    def second(self):
        for h in range(2):
            landed(self.take.at[h], self.sems[1].at[h])
            far = 1 - self.y if h == 0 else 1 - self.x
            self.pass_on[h] = self.joined(h, far).astype(jnp.bfloat16)
            push(
                self.pass_on.at[h], self.accept.at[h], self.sems[2].at[h], self.sems[3].at[h],
                self.across[1 - h],
            )

    def third(self, strip):
        for h in range(2):
            landed(self.accept.at[h], self.sems[3].at[h])
            near = self.y if h == 0 else self.x
            value = self.joined(h, near) + self.accept[h].astype(jnp.float32)
            strip[:, pl.ds(h * self.half, self.half)] = value.astype(jnp.bfloat16)
            landed(self.give.at[h], self.sems[0].at[h])
            landed(self.pass_on.at[h], self.sems[2].at[h])


def plane_scratch(rows, half):
    two = pltpu.VMEM((2, 2, rows, half), jnp.bfloat16)
    one = pltpu.VMEM((2, rows, half), jnp.bfloat16)
    return [two, two, two, one, one] + [pltpu.SemaphoreType.DMA((2,))] * 4


def relay_sems(beside):
    dma = pltpu.SemaphoreType.DMA
    base = [dma(()), dma((4,)), dma((4,)), dma((4,))] + [dma((2, 4))] * 4
    return base + ([dma((4,)), dma((4,))] + [dma((2, 4))] * 4 if beside else [])


def enter():
    me, core = lax.axis_index("dp"), lax.axis_index("mp")
    greet(*place_of(me), core)


def gather_kernel(block, table, out, tables, *sems):
    main = Relay(block, out, sems[:14], beside=True)
    small = Relay(table, tables, sems[14:22], paths=(0,))
    enter()
    main.start()
    small.start()
    for k in range(1, 4):
        main.step(k)
        small.step(k)
    main.each(3, main.second)
    small.each(3, small.second)
    for k in range(4):
        small.each(k, small.third)
    small.finish()
    for k in range(4):
        main.each(k, main.third)
    main.finish()


def params(number):
    return pltpu.CompilerParams(
        collective_id=number, has_side_effects=True, vmem_limit_bytes=48 * 1024 * 1024
    )


def gather_weight(block, table):
    rows, width = block.shape
    anywhere = pl.BlockSpec(memory_space=pl.ANY)
    out, tables = pl.pallas_call(
        gather_kernel,
        out_shape=(
            jax.ShapeDtypeStruct((4, 2, 2, rows, 2 * width), block.dtype),
            jax.ShapeDtypeStruct((4, 2, 2) + table.shape, table.dtype),
        ),
        in_specs=[anywhere] * 2,
        out_specs=(anywhere,) * 2,
        scratch_shapes=relay_sems(True) + relay_sems(False),
        compiler_params=params(0),
        cost_estimate=pl.CostEstimate(flops=0, bytes_accessed=100_000_000, transcendentals=0),
    )(block, table)
    tables = tables.reshape((16,) + table.shape).transpose(1, 0, 2).reshape(table.shape[0], -1)
    return out.reshape(16 * rows, 2 * width), tables


def times(left, weight, out):
    @pl.loop(0, weight.shape[1] // TILE)
    def _(j):
        span = pl.ds(pl.multiple_of(j * TILE, TILE), TILE)
        out[:, span] = jnp.dot(left[...], weight[:, span], preferred_element_type=jnp.float32)


def times_transposed(left, weight, out):
    @pl.loop(0, weight.shape[0] // TILE)
    def _(j):
        span = pl.ds(pl.multiple_of(j * TILE, TILE), TILE)
        out[:, span] = lax.dot_general(
            left[...], weight[span, :], (((1,), (1,)), ((), ())), preferred_element_type=jnp.float32
        )


def scale_of(state_f):
    return lax.rsqrt(jnp.mean(state_f * state_f, axis=-1, keepdims=True) + 1e-06)


def recur_kernel(
    state, levels, weight, cot_block, cot_sel, last_sel, final, grad, lefts, rights,
    xs, us, low, wide, dx, full, last, cot, cot_strip, last_strip, last_zone, end_strip, cot_zone, *sems
):
    cots, ends = Plane(*sems[:5], sems[5:9]), Plane(*sems[9:14], sems[14:18])
    line = Line(last_strip, last_zone, sems[18:22])
    cot_line = Line(cot_block, cot_zone, sems[22:26])
    lsend, lrecv, rsend, rrecv, esend, erecv = sems[26:]
    core, sibling = line.core, line.sibling
    part, strip, half = last.shape[0], last_strip.shape[1], rights.shape[3]
    mine = pl.ds(pl.multiple_of(core * strip, strip), strip)
    theirs = pl.ds(pl.multiple_of((1 - core) * strip, strip), strip)
    own_inner = pl.ds(pl.multiple_of(core * half, half), half)
    other_inner = pl.ds(pl.multiple_of((1 - core) * half, half), half)
    own_rows = pl.ds(pl.multiple_of(core * part, part), part)
    other_rows = pl.ds(pl.multiple_of((1 - core) * part, part), part)
    enter()
    cot_line.start()
    last[...] = state[...]
    for step in range(3):
        xs[step] = last[...]
        state_f = last[...].astype(jnp.float32)
        low[...] = (state_f * scale_of(state_f)).astype(jnp.bfloat16)
        times(low, weight, us.at[step])
        if step == 0:
            cot_line.step(1)
        if step == 1:
            cot_line.step(3)
            cot_line.finish()
            cots.first(cot_sel, cot_zone)
        if step == 2:
            cots.third(cot_strip)
            push(cot_strip.at[other_rows], cot.at[:, mine], esend.at[0], erecv.at[0], sibling)
            cot[:, mine] = cot_strip[own_rows, :]
        inner = us[step]
        low[...] = (inner / (1.0 + jnp.exp(-inner))).astype(jnp.bfloat16)
        times_transposed(low, weight, wide)
        active = (levels[...] >= step + 1).astype(jnp.float32)
        last[...] = (last[...].astype(jnp.float32) + active * wide[...]).astype(jnp.bfloat16)
        if step == 0:
            cot_line.step(2)
        if step == 1:
            cots.second()
    push(last.at[:, theirs], last_strip.at[own_rows], esend.at[1], erecv.at[1], sibling)
    last_strip[own_rows, :] = last[:, mine]
    landed(cot.at[:, theirs], erecv.at[0])
    dx[...] = cot[...].astype(jnp.float32)

    def share(i):
        push(lefts.at[core, i], lefts.at[core, i], lsend.at[i], lrecv.at[i], sibling)
        rights[core, i] = full[i, :, own_inner]
        push(full.at[i, :, other_inner], rights.at[core, i], rsend.at[i], rrecv.at[i], sibling)

    for step in (2, 1, 0):
        a, b = 2 * step, 2 * step + 1
        state_f = xs[step].astype(jnp.float32)
        rinv = scale_of(state_f)
        lefts[core, a] = (state_f * rinv).astype(jnp.bfloat16)
        active = (levels[...] >= step + 1).astype(jnp.float32)
        lefts[core, b] = (active * dx[...]).astype(jnp.bfloat16)
        times(lefts.at[core, b], weight, wide)
        if step == 2:
            landed(last_strip.at[other_rows], erecv.at[1])
            line.start()
        if step == 1:
            line.step(2)
        if step == 0:
            ends.second()
        inner = us[step]
        sigma = 1.0 / (1.0 + jnp.exp(-inner))
        full[b] = (inner * sigma).astype(jnp.bfloat16)
        full[a] = (wide[...] * sigma * (1.0 + inner * (1.0 - sigma))).astype(jnp.bfloat16)
        share(a)
        share(b)
        times_transposed(full.at[a], weight, wide)
        state_f = xs[step].astype(jnp.float32)
        mean = jnp.mean(wide[...] * state_f, axis=-1, keepdims=True)
        entry = dx[...] + rinv * wide[...] - state_f * (rinv * rinv * rinv * mean)
        dx[...] = entry.astype(jnp.bfloat16).astype(jnp.float32)
        if step == 2:
            line.step(1)
        if step == 1:
            line.step(3)
            line.finish()
            ends.first(last_sel, last_zone)
    grad[own_rows, :] = dx[...].astype(jnp.bfloat16)
    push(grad.at[own_rows], grad.at[own_rows], esend.at[2], erecv.at[2], sibling)
    ends.third(end_strip)
    push(end_strip, final.at[:, mine], esend.at[3], erecv.at[3], sibling)
    final[:, mine] = end_strip[...]
    for i in range(6):
        landed(lefts.at[1 - core, i], lrecv.at[i])
        landed(rights.at[1 - core, i], rrecv.at[i])
        landed(lefts.at[core, i], lsend.at[i])
        landed(full.at[i, :, other_inner], rsend.at[i])
    landed(cot_strip.at[other_rows], esend.at[0])
    landed(last.at[:, theirs], esend.at[1])
    landed(grad.at[own_rows], esend.at[2])
    landed(end_strip, esend.at[3])
    landed(grad.at[other_rows], erecv.at[2])
    landed(final.at[:, theirs], erecv.at[3])


def recur(state, levels, weight, cot_block, cot_sel, last_sel):
    part, width = state.shape
    rows, half, strip = 2 * part, weight.shape[1] // 2, width // 2
    vmem = pl.BlockSpec(memory_space=pltpu.VMEM)
    dma = pltpu.SemaphoreType.DMA
    low, high = jnp.bfloat16, jnp.float32
    final, grad, lefts, rights = pl.pallas_call(
        recur_kernel,
        out_shape=(
            jax.ShapeDtypeStruct((rows, width), low),
            jax.ShapeDtypeStruct((rows, width), low),
            jax.ShapeDtypeStruct((2, 6, part, width), low),
            jax.ShapeDtypeStruct((2, 6, part, half), low),
        ),
        in_specs=[vmem] * 6,
        out_specs=(vmem,) * 4,
        scratch_shapes=[
            pltpu.VMEM((3, part, width), low),
            pltpu.VMEM((3, part, 2 * half), high),
            pltpu.VMEM((part, 2 * half), low),
            pltpu.VMEM((part, width), high),
            pltpu.VMEM((part, width), high),
            pltpu.VMEM((6, part, 2 * half), low),
            pltpu.VMEM((part, width), low),
            pltpu.VMEM((part, width), low),
            pltpu.VMEM((rows, strip), low),
            pltpu.VMEM((rows, strip), low),
            pltpu.VMEM((4 * rows, strip), low),
            pltpu.VMEM((rows, strip), low),
            pltpu.VMEM((4 * rows, strip), low),
        ]
        + plane_scratch(rows, strip // 2) * 2
        + relay_sems(False)[:4] * 2
        + [dma((6,))] * 4
        + [dma((4,))] * 2,
        compiler_params=params(2),
    )(state, levels, weight, cot_block, cot_sel, last_sel)
    return final, grad, lefts.reshape(-1, width), rights.reshape(-1, half)


def scatter_kernel(
    left, right, out, d, btake, agive, atake, total, ugive, utake, dgive, dtake,
    bsend, brecv, asend, arecv, usend, urecv, dsend, drecv,
):
    me, core = lax.axis_index("dp"), lax.axis_index("mp")
    z, y, x = place_of(me)
    half = d.shape[4] // 2
    group = left.shape[1] // 4
    across = ((me + 1 - 2 * x, core), (me + 2 - 4 * y, core))
    greet(z, y, x, core)
    first = 3 * (1 - z // 2)
    third = 1 + z % 2
    order = (first, 6 - first - third - z, third, z)

    def cols(h):
        return pl.ds(h * half, half)

    for zp in order:
        span = pl.ds(pl.multiple_of(zp * group, group), group)
        product = lax.dot_general(
            left[:, span], right[...], (((0,), (0,)), ((), ())), preferred_element_type=jnp.float32
        )
        d[zp] = product.astype(d.dtype).reshape(d.shape[1:])
        push(d.at[zp, 1 - y, :, :, cols(0)], btake.at[0, zp], bsend.at[0, zp], brecv.at[0, zp], across[1])
        push(d.at[zp, :, 1 - x, :, cols(1)], btake.at[1, zp], bsend.at[1, zp], brecv.at[1, zp], across[0])

    def wide(value):
        return value.astype(jnp.float32)

    def middle(zp):
        for h in range(2):
            yp, xp, far, near = (y, 1 - x, 1 - x, x) if h == 0 else (1 - y, x, 1 - y, y)
            landed(btake.at[h, zp], brecv.at[h, zp])
            agive[h, zp] = (wide(d[zp, yp, xp, :, cols(h)]) + wide(btake[h, zp, far])).astype(d.dtype)
            push(agive.at[h, zp], atake.at[h, zp], asend.at[h, zp], arecv.at[h, zp], across[h])
            total[h, zp] = wide(d[zp, y, x, :, cols(h)]) + wide(btake[h, zp, near])

    def line(zp):
        for h in range(2):
            landed(atake.at[h, zp], arecv.at[h, zp])
            total[h, zp] += wide(atake[h, zp])

            @pl.when(zp > z)
            def _():
                @pl.when(z > 0)
                def _():
                    landed(utake.at[h, zp], urecv.at[h, zp])
                    total[h, zp] += wide(utake[h, zp])

                ugive[h, zp] = total[h, zp].astype(d.dtype)
                push(ugive.at[h, zp], utake.at[h, zp], usend.at[h, zp], urecv.at[h, zp], (me + 4, core))

            @pl.when(zp < z)
            def _():
                @pl.when(z < 3)
                def _():
                    landed(dtake.at[h, zp], drecv.at[h, zp])
                    total[h, zp] += wide(dtake[h, zp])

                dgive[h, zp] = total[h, zp].astype(d.dtype)
                push(dgive.at[h, zp], dtake.at[h, zp], dsend.at[h, zp], drecv.at[h, zp], (me - 4, core))

    middle(order[0])
    for k in range(1, 4):
        middle(order[k])
        line(order[k - 1])
    line(z)
    for h in range(2):

        @pl.when(z > 0)
        def _():
            landed(utake.at[h, z], urecv.at[h, z])
            total[h, z] += wide(utake[h, z])

        @pl.when(z < 3)
        def _():
            landed(dtake.at[h, z], drecv.at[h, z])
            total[h, z] += wide(dtake[h, z])

        out[:, cols(h)] = total[h, z]
    for zp in range(4):
        for h in range(2):
            landed(btake.at[h, zp], bsend.at[h, zp])
            landed(atake.at[h, zp], asend.at[h, zp])

            @pl.when(zp > z)
            def _():
                landed(ugive.at[h, zp], usend.at[h, zp])

            @pl.when(zp < z)
            def _():
                landed(dgive.at[h, zp], dsend.at[h, zp])


def scatter_grad(left, right):
    rows, width = left.shape[1] // 16, right.shape[1]
    half = width // 2
    dma = pltpu.SemaphoreType.DMA
    one = pltpu.VMEM((2, 4, rows, half), left.dtype)
    return pl.pallas_call(
        scatter_kernel,
        out_shape=jax.ShapeDtypeStruct((rows, width), jnp.float32),
        in_specs=[pl.BlockSpec(memory_space=pltpu.VMEM)] * 2,
        out_specs=pl.BlockSpec(memory_space=pltpu.VMEM),
        scratch_shapes=[
            pltpu.VMEM((4, 2, 2, rows, width), left.dtype),
            pltpu.VMEM((2, 4, 2, rows, half), left.dtype),
            one,
            one,
            pltpu.VMEM((2, 4, rows, half), jnp.float32),
            one,
            one,
            one,
            one,
        ]
        + [dma((2, 4))] * 8,
        compiler_params=pltpu.CompilerParams(
            collective_id=1, has_side_effects=True, vmem_limit_bytes=32 * 1024 * 1024
        ),
        cost_estimate=pl.CostEstimate(flops=0, bytes_accessed=100_000_000, transcendentals=0),
    )(left, right)


def pick(table, index):
    ids = lax.broadcasted_iota(jnp.int32, (index.shape[0], table.shape[0]), 1)
    return jnp.sum(jnp.where(ids == index[:, None], table[None, :], 0), axis=1)


def find(table, value):
    ids = lax.broadcasted_iota(jnp.int32, (value.shape[0], table.shape[0]), 1)
    return jnp.sum(jnp.where(table[None, :] == value[:, None], ids, 0), axis=1)


def take_rows(index, table):
    ids = lax.broadcasted_iota(jnp.int32, (index.shape[0], table.shape[0]), 1)
    return jnp.dot(
        (ids == index[:, None]).astype(jnp.bfloat16), table, preferred_element_type=jnp.float32
    ).astype(jnp.bfloat16)


def recursions(state, levels, cot, weight):
    saved = []
    for step in range(3):
        state_f = state.astype(jnp.float32)
        rinv = lax.rsqrt(jnp.mean(state_f * state_f, axis=-1, keepdims=True) + 1e-06)
        normed = (state_f * rinv).astype(jnp.bfloat16)
        inner = jnp.dot(normed, weight, preferred_element_type=jnp.float32)
        gated = jax.nn.silu(inner).astype(jnp.bfloat16)
        branch = lax.dot_general(
            gated, weight, (((1,), (1,)), ((), ())), preferred_element_type=jnp.float32
        )
        active = (levels >= step + 1).astype(jnp.float32)[:, None]
        saved.append((state_f, rinv, normed, inner, gated, active))
        state = (state_f + active * branch).astype(jnp.bfloat16)
    final = state
    grad = cot.astype(jnp.float32)
    lefts, rights = [], []
    for step in (2, 1, 0):
        state_f, rinv, normed, inner, gated, active = saved[step]
        grad_branch = (active * grad).astype(jnp.bfloat16)
        grad_gated = jnp.dot(grad_branch, weight, preferred_element_type=jnp.float32)
        sigma = jax.nn.sigmoid(inner)
        grad_inner = (grad_gated * sigma * (1.0 + inner * (1.0 - sigma))).astype(jnp.bfloat16)
        grad_normed = lax.dot_general(
            grad_inner, weight, (((1,), (1,)), ((), ())), preferred_element_type=jnp.float32
        )
        inner_mean = jnp.mean(grad_normed * state_f, axis=-1, keepdims=True)
        entry = grad + rinv * grad_normed - state_f * rinv * rinv * rinv * inner_mean
        lefts += [normed, grad_branch]
        rights += [grad_inner, gated]
        grad = entry.astype(jnp.bfloat16).astype(jnp.float32)
    return final, grad.astype(jnp.bfloat16), jnp.concatenate(lefts), jnp.concatenate(rights)


def from_column(position, rows, me):
    owner = position // rows
    return jnp.where(owner % 4 == me % 4, owner // 4 * rows + position % rows, -1)[:, None]


def body(hidden_in, depth, destination, weight, cotangent):
    rows, width = hidden_in.shape
    half_inner = weight.shape[1]
    cores = lax.axis_size("mp")
    me, core = lax.axis_index("dp"), lax.axis_index("mp")
    part, strip = rows // cores, width // cores
    state = lax.dynamic_slice_in_dim(hidden_in, core * part, part, 0)
    levels = lax.dynamic_slice_in_dim(depth, core * part, part, 0)
    cot_strip = lax.dynamic_slice_in_dim(cotangent, core * strip, strip, 1)
    contract = (((0,), (0,)), ((), ()))
    if lax.axis_size("dp") == 16 and cores == 2:
        full, tables = gather_weight(weight, destination)
        start = me // 4 * 4 * rows
        leaving = lax.dynamic_slice_in_dim(tables[0], start, 4 * rows, 0)
        place = pick(tables[2], pick(tables[1], leaving))
        own = start + jnp.arange(4 * rows, dtype=jnp.int32)
        source = find(tables[0], find(tables[1], find(tables[2], own)))
        final, grad_in, left_all, right_half = recur(
            state,
            levels.astype(jnp.float32)[:, None],
            full,
            cot_strip,
            from_column(place, rows, me),
            from_column(source, rows, me),
        )
        return final, grad_in, scatter_grad(left_all, right_half)
    columns = lax.all_gather(weight, "dp", axis=0, tiled=True)
    full = lax.all_gather(columns, "mp", axis=1, tiled=True)
    tables = lax.all_gather(destination, "dp", axis=1, tiled=True)
    cot_all = lax.all_gather(cot_strip, "dp", axis=0, tiled=True)
    place = pick(tables[2], pick(tables[1], destination[0]))
    own = me * rows + jnp.arange(rows, dtype=jnp.int32)
    source = find(tables[0], find(tables[1], find(tables[2], own)))
    cot_rows = lax.all_gather(take_rows(place, cot_all), "mp", axis=1, tiled=True)
    cot = lax.dynamic_slice_in_dim(cot_rows, core * part, part, 0)
    last, grad, left, right = recursions(state, levels, cot, full)
    last_all = lax.all_gather(last, "dp", axis=0, tiled=True)
    left_all = lax.all_gather(left, "mp", axis=0, tiled=True)
    right_all = lax.all_gather(right, "mp", axis=0, tiled=True)
    right_half = lax.dynamic_slice_in_dim(right_all, core * half_inner, half_inner, 1)
    owner, offset = source // rows, source % rows
    slot = jnp.where(offset // part == core, owner * part + offset % part, -1)
    final = lax.psum(take_rows(slot, last_all), "mp")
    grad_in = lax.all_gather(grad, "mp", axis=0, tiled=True)
    partial = lax.dot_general(
        left_all, right_half, contract, preferred_element_type=jnp.float32
    ).astype(jnp.bfloat16)
    owned = lax.psum_scatter(partial, "dp", scatter_dimension=0, tiled=True)
    return final, grad_in, owned.astype(jnp.float32)


def solution(mesh):
    placed = (P("dp", None), P("dp"), P(None, "dp"), P("dp", "mp"), P("dp", None))
    return jax.shard_map(
        body,
        mesh=mesh,
        in_specs=placed,
        out_specs=(P("dp", None), P("dp", None), P("dp", "mp")),
        check_vma=False,
    )
```
